1024 devices in a mesh: dp: 8 (over y), tensor: 16 (over z, core), expert: 8 (over x).
Axes of the slice: x: 8, y: 8, z: 8, core: 2. Of those that a mesh axis runs over, the one named last changes fastest.
Arguments:
- grad_out: bfloat16 [8, 8, 256, 4096], P('dp', 'expert', 'tensor'), may hold values from -6 to 6
- routes: int32 [8, 8, 256, 8], P('dp', 'expert'), may hold values from 0 to 63, all different within a row; in each aligned block of 256 rows (0 to 255, 256 to 511, ..., all dimensions but the last counted through in order) at most 48 rows name the same one
- gates: bfloat16 [8, 8, 256, 8], P('dp', 'expert'), may hold values from 0.049804688 to 1
- hidden_saved: bfloat16 [8, 64, 384, 768], P('dp', 'expert'), may hold values from -4 to 4
- w_down: bfloat16 [64, 768, 4096], P('expert', None, 'tensor'), may hold values from -0.09375 to 0.09375
Outputs:
- grad_hidden: bfloat16 [8, 64, 384, 768], P('dp', 'expert', 'tensor')
- grad_gates: float32 [8, 64, 384], P('dp', 'expert', 'tensor')
- grad_weight: bfloat16 [64, 768, 4096], P('expert', 'dp', 'tensor')
The draws below stay inside these ranges and needn't reach their ends.
Inputs may be any that keep to these rules, and one draw needn't show every extreme that they name: `routes`: within one column of 256 tokens each token names 8 different experts and no expert is named by more than 48 tokens; in every draw some expert is named by exactly 48 tokens of some column.
All inputs are finite; a program needn't handle non-finite values.
Results may differ from the reference program's by a relative error of at most 0.024.
Values may be sent and summed in bfloat16 or wider, within the bound.
No kernel may reach another device: no remote copies, remote signals or barrier semaphores. Data moves between devices by JAX's collectives and lax.ppermute only.
A program may use at most 128 MiB of HBM per device.

```python
import math
import jax
import jax.numpy as jnp
import numpy as np
from jax import lax

D = 4096
F = 768
TOPK = 8
EXPERTS = 64
GROUPS = 8
COLUMNS = 8
COL = 256
MOST = 48
SLOTS = 384
N_TENSOR = 16


def level_of(rng, shape, pieces, smallest, largest):
    level = 1.0
    for position, blocks in pieces:
        draws = jax.random.uniform(jax.random.fold_in(jax.random.fold_in(rng, 6), position), (blocks,), jnp.float32, smallest / len(pieces), largest / len(pieces))
        level = level * jnp.repeat(jnp.exp(draws), shape[position] // blocks).reshape((-1,) + (1,) * (len(shape) - 1 - position))
    return level


def shared_out(rng, own, number, rows, number_of, top, most, lean):
    order = jax.random.permutation(rng, number_of)
    packed, ordinary = shares(number_of, rows * top, most, lean, True), shares(number_of, rows * top, most, lean, False)
    places = jnp.arange(number_of)

    def named(tallies, turn):
        used = int((tallies > 0).sum())
        fixed = max(1, used // 4)
        moved = fixed + (places - fixed + turn * (used - fixed)) % max(1, number_of - fixed)
        return jnp.zeros((number_of,), jnp.int32).at[order[jnp.where(places < fixed, places, moved)]].set(jnp.asarray(tallies, jnp.int32))

    tallies = jnp.where(number % 4 == 0, named(packed, number // 4), named(ordinary, number - number // 4 - 1))
    mixed = jax.random.permutation(jax.random.fold_in(own, 3), number_of)
    giver, sink = mixed[0:number_of // 2 * 2:2], mixed[1:number_of // 2 * 2:2]
    room = jnp.minimum(tallies[giver] - 1, most - tallies[sink]) // 2
    room = jnp.where((giver == order[0]) | (sink == order[0]) | (tallies[sink] == 0), 0, jnp.maximum(room, 0))
    moved = jax.random.randint(jax.random.fold_in(own, 4), (number_of // 2,), 0, 1 << 20) % (room + 1)
    tallies = tallies.at[giver].add(-moved).at[sink].add(moved)
    labels = jnp.searchsorted(jnp.cumsum(tallies), jnp.arange(rows * top), side="right").astype(jnp.int32)
    table = labels.reshape(top, rows).T
    table = table[jax.random.permutation(jax.random.fold_in(own, 1), rows)]
    turn = jax.random.randint(jax.random.fold_in(own, 2), (rows, 1), 0, top)
    return jnp.take_along_axis(table, (jnp.arange(top)[None, :] + turn) % top, axis=1)


def shares(number_of, total, reach, skew, full):
    weights = [(1 << 20) // math.isqrt(rank ** skew) + 1 for rank in range(1, number_of + 1)]
    largest = reach if full else min(reach, max(-(-total // number_of), total * weights[0] // sum(weights)))
    least = 1 if total - largest >= number_of - 1 else 0
    counts, surplus = [largest] + [least] * (number_of - 1), total - largest - least * (number_of - 1)
    while surplus > 0:
        movable = [i for i in range(1, number_of) if counts[i] < largest] or [i for i in range(1, number_of) if counts[i] < reach]
        whole, budget = sum([weights[i] for i in movable]), surplus
        for i in movable:
            extra = min(reach - counts[i], max(1, budget * weights[i] // whole), surplus)
            counts[i] = counts[i] + extra
            surplus = surplus - extra
    return np.array(counts)


def noise(stream_key, extent, scale, most, pieces=(), kind=jnp.bfloat16):
    drawn = scale * jax.random.normal(stream_key, extent, jnp.float32)
    if pieces:
        drawn = drawn * level_of(stream_key, extent, pieces, -0.22, 0.18)
    return jnp.clip(drawn, -most, most).astype(kind)


def setup_inputs(seed: int = 0) -> dict:
    seeds = jax.random.split(jax.random.key(seed), 6)
    grad_out = noise(seeds[0], (GROUPS, COLUMNS, COL, D), 1.0, 6.0, ((0, 8), (1, 8), (2, 16)))
    routes_keys = jax.random.split(jax.random.fold_in(seeds[1], 1), GROUPS * COLUMNS * COL // COL)
    routes_turns = jax.random.permutation(jax.random.fold_in(seeds[1], 3), GROUPS * COLUMNS * COL // COL)
    routes = jax.vmap(lambda own, number: shared_out(jax.random.fold_in(seeds[1], 2), own, number, COL, EXPERTS, TOPK, MOST, 2))(routes_keys, routes_turns).reshape((GROUPS, COLUMNS, COL, TOPK))
    gates = jnp.clip(0.049804688 + 0.9501953 * jax.random.uniform(seeds[2], (GROUPS, COLUMNS, COL, TOPK), jnp.float32) ** level_of(seeds[2], (GROUPS, COLUMNS, COL, TOPK), ((0, 8), (1, 8)), -0.2, 0.2), 0.049804688, 1.0).astype(jnp.bfloat16)
    hidden_saved = noise(seeds[3], (GROUPS, EXPERTS, SLOTS, F), 0.5, 4.0, ((0, 8), (1, 8)))
    w_down = noise(seeds[4], (EXPERTS, F, D), D ** -0.5, 0.09375, ((0, 8), (2, 16)))
    return dict(grad_out=grad_out, routes=routes, gates=gates, hidden_saved=hidden_saved, w_down=w_down)


def slot_ranks(route_col):
    onehot = (route_col[:, :, None] == jnp.arange(EXPERTS, dtype=jnp.int32)[None, None, :]).astype(jnp.int32)
    named = jnp.sum(onehot, axis=1)
    before = jnp.cumsum(named, axis=0) - named
    return jnp.sum(onehot * before[:, None, :], axis=2).astype(jnp.int32)


def group_buffers(grad_group, route_group, gate_group):
    ranks = jax.vmap(slot_ranks)(route_group)
    column_base = (jnp.arange(COLUMNS, dtype=jnp.int32) * MOST)[:, None, None]
    slot_index = (column_base + ranks).reshape(-1)
    expert_index = route_group.reshape(-1)
    rows = jnp.broadcast_to(grad_group[:, :, None, :], (COLUMNS, COL, TOPK, D)).reshape(-1, D)
    slot_rows = jnp.zeros((EXPERTS, SLOTS, D), jnp.bfloat16).at[expert_index, slot_index].set(rows)
    slot_gates = jnp.zeros((EXPERTS, SLOTS), jnp.float32).at[expert_index, slot_index].set(gate_group.reshape(-1).astype(jnp.float32))
    return slot_rows, slot_gates


def expert_work(item):
    rows, gate_col, hidden, weight = item
    width_block = D // N_TENSOR
    rows_split = rows.astype(jnp.float32).reshape(SLOTS, N_TENSOR, width_block)
    weight_split = weight.astype(jnp.float32).reshape(F, N_TENSOR, width_block)
    parts = jnp.einsum("snd,fnd->nsf", rows_split, weight_split)
    parts = lax.optimization_barrier(parts.astype(jnp.bfloat16)).astype(jnp.float32)
    values = jnp.sum(parts, axis=0)
    grad_hidden = (gate_col[:, None] * values).astype(jnp.bfloat16)
    grad_gates = jnp.sum(hidden.astype(jnp.float32) * values, axis=1)
    scaled = (gate_col[:, None] * rows.astype(jnp.float32)).astype(jnp.bfloat16)
    group_part = jnp.einsum("sf,sd->fd", hidden.astype(jnp.float32), scaled.astype(jnp.float32)).astype(jnp.bfloat16)
    return grad_hidden, grad_gates, group_part


def reference(grad_out, routes, gates, hidden_saved, w_down):
    def one_group(total, group):
        grad_group, route_group, gate_group, hidden_group = group
        slot_rows, slot_gates = group_buffers(grad_group, route_group, gate_group)
        grad_hidden, grad_gates, group_part = lax.map(expert_work, (slot_rows, slot_gates, hidden_group, w_down))
        group_part = lax.optimization_barrier(group_part)
        return total + group_part.astype(jnp.float32), (grad_hidden, grad_gates)

    start = jnp.zeros((EXPERTS, F, D), jnp.float32)
    total, (grad_hidden, grad_gates) = lax.scan(one_group, start, (grad_out, routes, gates, hidden_saved))
    return grad_hidden, grad_gates, total.astype(jnp.bfloat16)
```

```python
import functools

import jax
import jax.numpy as jnp
from jax import lax
from jax.experimental import pallas as pl
from jax.experimental.pallas import tpu as pltpu
from jax.sharding import PartitionSpec as P

BF = jnp.bfloat16
F32 = jnp.float32


def iota(shape, dim):
    return lax.broadcasted_iota(jnp.int32, shape, dim)


def tables(arr_ref, columns, first, experts, tokens, choices):
    expert_of = (first + iota((experts, tokens), 0)).astype(F32)
    named, gates = [], []
    for c in columns:
        meta = arr_ref[c, tokens : tokens + 2 * choices, :].astype(F32)
        hit_any = jnp.zeros((experts, tokens), F32)
        gate = jnp.zeros((experts, tokens), F32)
        for k in range(choices):
            hit = meta[k : k + 1, :] == expert_of
            hit_any = jnp.where(hit, 1.0, hit_any)
            gate = jnp.where(hit, meta[choices + k : choices + k + 1, :], gate)
        named.append(hit_any)
        gates.append(gate)
    named = jnp.concatenate(named, 0)
    before = (iota((tokens, tokens), 0) < iota((tokens, tokens), 1)).astype(F32).astype(BF)
    rank = jnp.dot(named.astype(BF), before, preferred_element_type=F32)
    table = jnp.where(named > 0, rank, -1.0)
    return [table[i * experts : (i + 1) * experts] for i in range(len(gates))], gates


def picker(table, gate, base, slots, experts, tokens):
    rank = (base + iota((slots, tokens), 0)).astype(F32)
    rows = []
    for x in range(experts):
        value = 1.0 if gate is None else gate[x : x + 1, :]
        rows.append(jnp.where(table[x : x + 1, :] == rank, value, 0.0))
    return jnp.concatenate(rows, 0)


def weight_kernel(place, arr_ref, hidden_ref, out_ref, scaled, *, dims):
    experts, columns, tokens, choices, most = dims
    step = pl.program_id(0)

    @pl.when(step == 0)
    def _():
        table, gates = tables(arr_ref, range(columns), place[0] * experts, experts, tokens, choices)
        for c in range(columns):
            pick = picker(table[c], gates[c], 0, most, experts, tokens).astype(BF)
            rows = jnp.dot(pick, arr_ref[c, :tokens, :], preferred_element_type=F32).astype(BF)
            for x in range(experts):
                scaled[x, c * most : (c + 1) * most, :] = rows[x * most : (x + 1) * most]

    part = lax.dot_general(
        hidden_ref[0], scaled[step], (((0,), (0,)), ((), ())), preferred_element_type=F32
    )
    out_ref[:, 0] = part.astype(BF).reshape(out_ref.shape[0], out_ref.shape[2], out_ref.shape[3])


def part_kernel(place, arr_ref, other_ref, w_ref, w_other_ref, out_ref, gate_ref, mine, theirs, *, dims):
    experts, columns, tokens, choices, most = dims
    half = most // 2
    step = pl.program_id(0)

    @pl.when(step == 0)
    def _():
        base = place[2] * half
        first = place[0] * experts
        table, _ = tables(arr_ref, range(columns), first, experts, tokens, choices)
        for c in range(columns):
            pick = picker(table[c], None, base, half, experts, tokens).astype(BF)
            for src, dst in ((arr_ref, mine), (other_ref, theirs)):
                rows = jnp.dot(pick, src[c, :tokens, :], preferred_element_type=F32)
                for x in range(experts):
                    dst[x, c * half : (c + 1) * half, :] = rows[x * half : (x + 1) * half]
        own, gates = tables(arr_ref, [place[1]], first, experts, tokens, choices)
        gate = picker(own[0], gates[0], base, half, experts, tokens)
        gate_ref[...] = jnp.broadcast_to(jnp.sum(gate, axis=1, keepdims=True), gate_ref.shape)

    dims_nt = (((1,), (1,)), ((), ()))
    part = lax.dot_general(mine[step].astype(BF), w_ref[0], dims_nt, preferred_element_type=F32)
    part = part + lax.dot_general(
        theirs[step].astype(BF), w_other_ref[0], dims_nt, preferred_element_type=F32
    )
    out_ref[:, 0] = part.astype(BF).reshape(columns, half, part.shape[1])


def finish_kernel(parts_ref, gate_ref, hidden_ref, grad_ref, gates_ref):
    sources, experts, half, width = parts_ref.shape
    values = parts_ref[0].astype(F32)
    for s in range(1, sources):
        values = values + parts_ref[s].astype(F32)
    gate = gate_ref[:, :1].reshape(experts, half, 1)
    grad_ref[...] = (gate * values).astype(BF)
    gates_ref[...] = jnp.sum(hidden_ref[...].astype(F32) * values, axis=2)


def local(grad_out, routes, gates, hidden_saved, w_down):
    n_tensor = lax.axis_size("tensor")
    n_expert = lax.axis_size("expert")
    n_dp = lax.axis_size("dp")
    chips = n_tensor // 2
    experts, width, block = w_down.shape
    slots = hidden_saved.shape[2]
    most = slots // n_expert
    half = most // 2
    tokens, choices = routes.shape[2:]
    own = grad_out.shape[2]
    dims = (experts, n_expert, tokens, choices, most)
    me = lax.axis_index("tensor")
    place = jnp.stack([lax.axis_index("expert"), me // 2, me % 2]).astype(jnp.int32)
    pair = [(i, i ^ 1) for i in range(n_tensor)]
    params = functools.partial(pltpu.CompilerParams, vmem_limit_bytes=32 * 1024 * 1024)

    w_other = lax.ppermute(w_down, "tensor", pair)
    first = me * (slots // n_tensor)
    my_hidden = lax.dynamic_slice_in_dim(hidden_saved[0], first, slots // n_tensor, 1)

    send = grad_out[0, 0].reshape(own, n_tensor, block).transpose(1, 0, 2)
    column = lax.all_to_all(send, "tensor", 0, 0, tiled=True).reshape(tokens, block)
    packed = jnp.concatenate([column, routes[0, 0].T.astype(BF), gates[0, 0].T], 0)
    packed = jnp.broadcast_to(packed[None], (n_expert,) + packed.shape)
    arr = lax.all_to_all(packed, "expert", 0, 0, tiled=True)
    other = lax.ppermute(arr, "tensor", pair)

    rows_all = arr.shape[1]
    whole = lambda *shape: pl.BlockSpec(shape, lambda x, p: (0,) * len(shape))
    per_expert = lambda *shape: pl.BlockSpec((1,) + shape, lambda x, p: (x, 0, 0))
    block_f = width // n_dp
    partial = pl.pallas_call(
        functools.partial(weight_kernel, dims=dims),
        out_shape=jax.ShapeDtypeStruct((n_dp, experts, block_f, block), BF),
        grid_spec=pltpu.PrefetchScalarGridSpec(
            num_scalar_prefetch=1,
            grid=(experts,),
            in_specs=[whole(n_expert, rows_all, block), per_expert(slots, width)],
            out_specs=pl.BlockSpec((n_dp, 1, block_f, block), lambda x, p: (0, x, 0, 0)),
            scratch_shapes=[pltpu.VMEM((experts, slots, block), BF)],
        ),
        compiler_params=params(),
        name="weight_part",
    )(place, arr, hidden_saved[0])
    total = lax.psum_scatter(partial, "dp", scatter_dimension=0, tiled=True)[0]

    arr_after, _ = lax.optimization_barrier((arr, partial))
    parts, gate_col = pl.pallas_call(
        functools.partial(part_kernel, dims=dims),
        out_shape=(
            jax.ShapeDtypeStruct((n_expert, experts, half, width), BF),
            jax.ShapeDtypeStruct((experts * half, 128), F32),
        ),
        grid_spec=pltpu.PrefetchScalarGridSpec(
            num_scalar_prefetch=1,
            grid=(experts,),
            in_specs=[
                whole(n_expert, rows_all, block),
                whole(n_expert, rows_all, block),
                per_expert(width, block),
                per_expert(width, block),
            ],
            out_specs=(
                pl.BlockSpec((n_expert, 1, half, width), lambda x, p: (0, x, 0, 0)),
                whole(experts * half, 128),
            ),
            scratch_shapes=[pltpu.VMEM((experts, slots // 2, block), F32)] * 2,
        ),
        compiler_params=params(),
        name="hidden_part",
    )(place, arr_after, other, w_down, w_other)
    same_core = [[2 * z + c for z in range(chips)] for c in range(2)]
    parts = lax.all_to_all(parts, "tensor", 0, 0, tiled=True, axis_index_groups=same_core)
    grad_hidden, grad_gates = pl.pallas_call(
        finish_kernel,
        out_shape=(
            jax.ShapeDtypeStruct((experts, half, width), BF),
            jax.ShapeDtypeStruct((experts, half), F32),
        ),
        in_specs=[pl.BlockSpec(memory_space=pltpu.VMEM)] * 3,
        out_specs=(pl.BlockSpec(memory_space=pltpu.VMEM),) * 2,
        compiler_params=params(),
        name="finish",
    )(parts, gate_col, my_hidden)
    return grad_hidden[None], grad_gates[None], total


def solution(mesh):
    in_specs = (
        P("dp", "expert", "tensor", None),
        P("dp", "expert", None, None),
        P("dp", "expert", None, None),
        P("dp", "expert", None, None),
        P("expert", None, "tensor"),
    )
    out_specs = (
        P("dp", "expert", "tensor", None),
        P("dp", "expert", "tensor"),
        P("expert", "dp", "tensor"),
    )
    return jax.shard_map(local, mesh=mesh, in_specs=in_specs, out_specs=out_specs, check_vma=False)
```

```python
import functools

import jax
import jax.numpy as jnp
from jax import lax
from jax.experimental import pallas as pl
from jax.experimental.pallas import tpu as pltpu
from jax.sharding import PartitionSpec as P

BF = jnp.bfloat16
F32 = jnp.float32


def iota(shape, dim):
    return lax.broadcasted_iota(jnp.int32, shape, dim)


def tables(few_ref, columns, core, first, experts, tokens, choices):
    expert_of = (first + iota((experts, tokens), 0)).astype(F32)
    head = few_ref.shape[1] - 2 * choices
    n_columns = few_ref.shape[0] // 2
    named, gates = [], []
    for c in columns:
        meta = few_ref[core * n_columns + c, head:, :].astype(F32)
        hit_any = jnp.zeros((experts, tokens), F32)
        gate = jnp.zeros((experts, tokens), F32)
        for k in range(choices):
            hit = meta[k : k + 1, :] == expert_of
            hit_any = jnp.where(hit, 1.0, hit_any)
            gate = jnp.where(hit, meta[choices + k : choices + k + 1, :], gate)
        named.append(hit_any)
        gates.append(gate)
    named = jnp.concatenate(named, 0)
    before = (iota((tokens, tokens), 0) < iota((tokens, tokens), 1)).astype(F32).astype(BF)
    rank = jnp.dot(named.astype(BF), before, preferred_element_type=F32)
    table = jnp.where(named > 0, rank, -1.0)
    return [table[i * experts : (i + 1) * experts] for i in range(len(gates))], gates


def column_tokens(many_ref, few_ref, c, core, choices):
    head = few_ref.shape[1] - 2 * choices
    few = few_ref[core * (few_ref.shape[0] // 2) + c, :head, :]
    return jnp.concatenate([many_ref[c], few], 0)


def picker(table, gate, base, slots, experts, tokens):
    rank = (base + iota((slots, tokens), 0)).astype(F32)
    rows = []
    for x in range(experts):
        value = 1.0 if gate is None else gate[x : x + 1, :]
        rows.append(jnp.where(table[x : x + 1, :] == rank, value, 0.0))
    return jnp.concatenate(rows, 0)


def weight_kernel(place, many_ref, few_ref, hidden_ref, out_ref, scaled, *, dims):
    experts, columns, tokens, choices, most = dims
    step = pl.program_id(0)

    @pl.when(step == 0)
    def _():
        first = place[0] * experts
        table, gates = tables(few_ref, range(columns), place[2], first, experts, tokens, choices)
        for c in range(columns):
            pick = picker(table[c], gates[c], 0, most, experts, tokens).astype(BF)
            column = column_tokens(many_ref, few_ref, c, place[2], choices)
            rows = jnp.dot(pick, column, preferred_element_type=F32).astype(BF)
            for x in range(experts):
                scaled[x, c * most : (c + 1) * most, :] = rows[x * most : (x + 1) * most]

    part = lax.dot_general(
        hidden_ref[0], scaled[step], (((0,), (0,)), ((), ())), preferred_element_type=F32
    )
    out_ref[:, 0] = part.astype(BF).reshape(out_ref.shape[0], out_ref.shape[2], out_ref.shape[3])


def part_kernel(
    place, many_ref, other_ref, few_ref, w_ref, w_other_ref, out_ref, gate_ref, mine, theirs, *, dims
):
    experts, columns, tokens, choices, most = dims
    half = most // 2
    step = pl.program_id(0)

    @pl.when(step == 0)
    def _():
        core = place[2]
        base = core * half
        first = place[0] * experts
        table, _ = tables(few_ref, range(columns), core, first, experts, tokens, choices)
        for c in range(columns):
            pick = picker(table[c], None, base, half, experts, tokens).astype(BF)
            for src, of_core, dst in ((many_ref, core, mine), (other_ref, 1 - core, theirs)):
                column = column_tokens(src, few_ref, c, of_core, choices)
                rows = jnp.dot(pick, column, preferred_element_type=F32)
                for x in range(experts):
                    dst[x, c * half : (c + 1) * half, :] = rows[x * half : (x + 1) * half]
        own, gates = tables(few_ref, [place[1]], core, first, experts, tokens, choices)
        gate = picker(own[0], gates[0], base, half, experts, tokens)
        gate_ref[...] = jnp.broadcast_to(jnp.sum(gate, axis=1, keepdims=True), gate_ref.shape)

    dims_nt = (((1,), (1,)), ((), ()))
    part = lax.dot_general(mine[step].astype(BF), w_ref[0], dims_nt, preferred_element_type=F32)
    part = part + lax.dot_general(
        theirs[step].astype(BF), w_other_ref[0], dims_nt, preferred_element_type=F32
    )
    out_ref[:, 0] = part.astype(BF).reshape(columns, half, part.shape[1])


def finish_kernel(parts_ref, gate_ref, hidden_ref, grad_ref, gates_ref):
    sources, experts, half, width = parts_ref.shape
    values = parts_ref[0].astype(F32)
    for s in range(1, sources):
        values = values + parts_ref[s].astype(F32)
    gate = gate_ref[:, :1].reshape(experts, half, 1)
    grad_ref[...] = (gate * values).astype(BF)
    gates_ref[...] = jnp.sum(hidden_ref[...].astype(F32) * values, axis=2)


def local(grad_out, routes, gates, hidden_saved, w_down):
    n_tensor = lax.axis_size("tensor")
    n_expert = lax.axis_size("expert")
    n_dp = lax.axis_size("dp")
    chips = n_tensor // 2
    experts, width, block = w_down.shape
    slots = hidden_saved.shape[2]
    most = slots // n_expert
    half = most // 2
    tokens, choices = routes.shape[2:]
    own = grad_out.shape[2]
    dims = (experts, n_expert, tokens, choices, most)
    me = lax.axis_index("tensor")
    place = jnp.stack([lax.axis_index("expert"), me // 2, me % 2]).astype(jnp.int32)
    pair = [(i, i ^ 1) for i in range(n_tensor)]
    params = pltpu.CompilerParams(vmem_limit_bytes=60 * 1024 * 1024)

    work = 2 * experts * slots * width * block + 2 * n_expert * slots * tokens * block
    cost = pl.CostEstimate(flops=work, bytes_accessed=2 * w_down.size, transcendentals=0)

    w_other = lax.ppermute(w_down, "tensor", pair)
    first = me * (slots // n_tensor)
    my_hidden = lax.dynamic_slice_in_dim(hidden_saved[0], first, slots // n_tensor, 1)

    send = grad_out[0, 0].reshape(own, n_tensor, block).transpose(1, 0, 2)
    column = lax.all_to_all(send, "tensor", 0, 0, tiled=True).reshape(tokens, block)
    cut = tokens - own
    few = jnp.concatenate([column[cut:], routes[0, 0].T.astype(BF), gates[0, 0].T], 0)
    few = jnp.broadcast_to(few[None], (2 * n_expert,) + few.shape)
    same_chip = [
        [(2 * z + c) * n_expert + x for c in range(2) for x in range(n_expert)] for z in range(chips)
    ]
    few = lax.all_to_all(
        few, ("tensor", "expert"), 0, 0, tiled=True, axis_index_groups=same_chip
    )
    many = lax.all_gather(column[:cut], "expert")
    many, few = lax.optimization_barrier((many, few))
    other = lax.ppermute(many, "tensor", pair)

    whole = lambda *shape: pl.BlockSpec(shape, lambda x, p: (0,) * len(shape))
    per_expert = lambda *shape: pl.BlockSpec((1,) + shape, lambda x, p: (x, 0, 0))
    block_f = width // n_dp
    parts, gate_col = pl.pallas_call(
        functools.partial(part_kernel, dims=dims),
        out_shape=(
            jax.ShapeDtypeStruct((n_expert, experts, half, width), BF),
            jax.ShapeDtypeStruct((experts * half, 128), F32),
        ),
        grid_spec=pltpu.PrefetchScalarGridSpec(
            num_scalar_prefetch=1,
            grid=(experts,),
            in_specs=[
                whole(*many.shape),
                whole(*many.shape),
                whole(*few.shape),
                per_expert(width, block),
                per_expert(width, block),
            ],
            out_specs=(
                pl.BlockSpec((n_expert, 1, half, width), lambda x, p: (0, x, 0, 0)),
                whole(experts * half, 128),
            ),
            scratch_shapes=[pltpu.VMEM((experts, slots // 2, block), F32)] * 2,
        ),
        compiler_params=params,
        cost_estimate=cost,
        name="hidden_part",
    )(place, many, other, few, w_down, w_other)

    partial = pl.pallas_call(
        functools.partial(weight_kernel, dims=dims),
        out_shape=jax.ShapeDtypeStruct((n_dp, experts, block_f, block), BF),
        grid_spec=pltpu.PrefetchScalarGridSpec(
            num_scalar_prefetch=1,
            grid=(experts,),
            in_specs=[whole(*many.shape), whole(*few.shape), per_expert(slots, width)],
            out_specs=pl.BlockSpec((n_dp, 1, block_f, block), lambda x, p: (0, x, 0, 0)),
            scratch_shapes=[pltpu.VMEM((experts, slots, block), BF)],
        ),
        compiler_params=params,
        cost_estimate=cost,
        name="weight_part",
    )(place, many, few, hidden_saved[0])
    total = lax.psum_scatter(partial, "dp", scatter_dimension=0, tiled=True)[0]

    same_core = [[2 * z + c for z in range(chips)] for c in range(2)]
    parts = lax.all_to_all(parts, "tensor", 0, 0, tiled=True, axis_index_groups=same_core)
    grad_hidden, grad_gates = pl.pallas_call(
        finish_kernel,
        out_shape=(
            jax.ShapeDtypeStruct((experts, half, width), BF),
            jax.ShapeDtypeStruct((experts, half), F32),
        ),
        in_specs=[pl.BlockSpec(memory_space=pltpu.VMEM)] * 3,
        out_specs=(pl.BlockSpec(memory_space=pltpu.VMEM),) * 2,
        compiler_params=pltpu.CompilerParams(vmem_limit_bytes=32 * 1024 * 1024),
        name="finish",
    )(parts, gate_col, my_hidden)
    return grad_hidden[None], grad_gates[None], total


def solution(mesh):
    in_specs = (
        P("dp", "expert", "tensor", None),
        P("dp", "expert", None, None),
        P("dp", "expert", None, None),
        P("dp", "expert", None, None),
        P("expert", None, "tensor"),
    )
    out_specs = (
        P("dp", "expert", "tensor", None),
        P("dp", "expert", "tensor"),
        P("expert", "dp", "tensor"),
    )
    return jax.shard_map(local, mesh=mesh, in_specs=in_specs, out_specs=out_specs, check_vma=False)
```

```python
import functools

import jax
import jax.numpy as jnp
from jax import lax
from jax.experimental import pallas as pl
from jax.experimental.pallas import tpu as pltpu
from jax.sharding import PartitionSpec as P

BF = jnp.bfloat16
F32 = jnp.float32


def iota(shape, dim):
    return lax.broadcasted_iota(jnp.int32, shape, dim)


def tables(meta_ref, columns, first, experts, tokens, choices):
    expert_of = (first + iota((experts, tokens), 0)).astype(F32)
    named, gates = [], []
    for c in range(columns):
        meta = meta_ref[c].astype(F32)
        hit_any = jnp.zeros((experts, tokens), F32)
        gate = jnp.zeros((experts, tokens), F32)
        for k in range(choices):
            hit = meta[k : k + 1, :] == expert_of
            hit_any = jnp.where(hit, 1.0, hit_any)
            gate = jnp.where(hit, meta[choices + k : choices + k + 1, :], gate)
        named.append(hit_any)
        gates.append(gate)
    named = jnp.concatenate(named, 0)
    before = (iota((tokens, tokens), 0) < iota((tokens, tokens), 1)).astype(F32).astype(BF)
    rank = jnp.dot(named.astype(BF), before, preferred_element_type=F32)
    table = jnp.where(named > 0, rank, -1.0)
    return [table[c * experts : (c + 1) * experts] for c in range(columns)], gates


def picker(table, gate, base, slots, experts, tokens):
    rank = (base + iota((slots, tokens), 0)).astype(F32)
    rows = []
    for x in range(experts):
        value = 1.0 if gate is None else gate[x : x + 1, :]
        rows.append(jnp.where(table[x : x + 1, :] == rank, value, 0.0))
    return jnp.concatenate(rows, 0)


def weight_kernel(place, tok_ref, meta_ref, hidden_ref, out_ref, hot_ref, gate_ref, scaled, *, dims):
    experts, columns, tokens, choices, most = dims
    half = most // 2
    step = pl.program_id(0)
    per = hidden_ref.shape[0]

    @pl.when(step == 0)
    def _():
        table, gates = tables(meta_ref, columns, place[0] * experts, experts, tokens, choices)
        for c in range(columns):
            pick = picker(table[c], gates[c], 0, most, experts, tokens).astype(BF)
            rows = jnp.dot(pick, tok_ref[c], preferred_element_type=F32).astype(BF)
            for x in range(experts):
                scaled[x, c * most : (c + 1) * most, :] = rows[x * most : (x + 1) * most]
            base = place[2] * half
            hot_ref[c] = picker(table[c], None, base, half, experts, tokens).astype(BF)

            @pl.when(place[1] == c)
            def _():
                gate = picker(table[c], gates[c], base, half, experts, tokens)
                gate_ref[...] = jnp.broadcast_to(
                    jnp.sum(gate, axis=1, keepdims=True), gate_ref.shape
                )

    for i in range(per):
        part = lax.dot_general(
            hidden_ref[i],
            scaled[step * per + i],
            (((0,), (0,)), ((), ())),
            preferred_element_type=F32,
        )
        n_dp, _, block_f, block = out_ref.shape
        out_ref[:, i] = part.astype(BF).reshape(n_dp, block_f, block)


def part_kernel(
    place, tok_ref, other_ref, hot_ref, w_ref, w_other_ref, keep_ref, near_ref, far_ref, mine, theirs
):
    columns, rows_half, _ = hot_ref.shape
    experts = mine.shape[0]
    half = rows_half // experts
    step = pl.program_id(0)
    per = w_ref.shape[0]

    @pl.when(step == 0)
    def _():
        for c in range(columns):
            for src, dst in ((tok_ref, mine), (other_ref, theirs)):
                rows = jnp.dot(hot_ref[c], src[c], preferred_element_type=F32)
                for x in range(experts):
                    dst[x, c * half : (c + 1) * half, :] = rows[x * half : (x + 1) * half]

    dims_nt = (((1,), (1,)), ((), ()))
    odd = place[1] % 2 == 1
    for i in range(per):
        x = step * per + i
        part = lax.dot_general(mine[x].astype(BF), w_ref[i], dims_nt, preferred_element_type=F32)
        part = part + lax.dot_general(
            theirs[x].astype(BF), w_other_ref[i], dims_nt, preferred_element_type=F32
        )
        part = part.reshape(columns // 2, 2, half, part.shape[1])
        keep_ref[:, i] = jnp.where(odd, part[:, 1], part[:, 0]).astype(BF)
        give = jnp.where(odd, part[:, 0], part[:, 1]).astype(BF)

        @pl.when(x < experts // 2)
        def _():
            near_ref[:, i] = give

        @pl.when(x >= experts // 2)
        def _():
            far_ref[:, i] = give


def add_kernel(keep_ref, near_ref, far_ref, out_ref):
    h = near_ref.shape[1]
    out_ref[:, :h] = (keep_ref[:, :h].astype(F32) + near_ref[...].astype(F32)).astype(BF)
    out_ref[:, h:] = (keep_ref[:, h:].astype(F32) + far_ref[...].astype(F32)).astype(BF)


def finish_kernel(parts_ref, gate_ref, hidden_ref, grad_ref, gates_ref):
    sources, experts, half, width = parts_ref.shape
    values = parts_ref[0].astype(F32)
    for s in range(1, sources):
        values = values + parts_ref[s].astype(F32)
    gate = gate_ref[:, :1].reshape(experts, half, 1)
    grad_ref[...] = (gate * values).astype(BF)
    gates_ref[...] = jnp.sum(hidden_ref[...].astype(F32) * values, axis=2)


def local(grad_out, routes, gates, hidden_saved, w_down):
    n_tensor = lax.axis_size("tensor")
    n_expert = lax.axis_size("expert")
    n_dp = lax.axis_size("dp")
    chips = n_tensor // 2
    experts, width, block = w_down.shape
    slots = hidden_saved.shape[2]
    most = slots // n_expert
    half = most // 2
    tokens, choices = routes.shape[2:]
    own = grad_out.shape[2]
    dims = (experts, n_expert, tokens, choices, most)
    me = lax.axis_index("tensor")
    place = jnp.stack([lax.axis_index("expert"), me // 2, me % 2]).astype(jnp.int32)
    pair = [(i, i ^ 1) for i in range(n_tensor)]
    params = pltpu.CompilerParams(vmem_limit_bytes=50 * 1024 * 1024)

    work = 2 * experts * slots * width * block + 2 * n_expert * slots * tokens * block
    cost = pl.CostEstimate(flops=work, bytes_accessed=2 * w_down.size, transcendentals=0)

    w_other = lax.ppermute(w_down, "tensor", pair)
    first = me * (slots // n_tensor)
    my_hidden = lax.dynamic_slice_in_dim(hidden_saved[0], first, slots // n_tensor, 1)

    meta = jnp.concatenate([routes[0, 0].T.astype(BF), gates[0, 0].T], 0)
    meta, w_other = lax.optimization_barrier((lax.all_gather(meta, "expert"), w_other))
    send = grad_out[0, 0].reshape(own, n_tensor, block).transpose(1, 0, 2)
    send = jnp.broadcast_to(send[None], (n_expert,) + send.shape)
    send = send.reshape(n_expert * n_tensor, own, block)
    tok = lax.all_to_all(send, ("expert", "tensor"), 0, 0, tiled=True)
    tok = tok.reshape(n_expert, tokens, block)
    other = lax.ppermute(tok, "tensor", pair)

    per = 2
    whole = lambda *shape: pl.BlockSpec(shape, lambda x, p: (0,) * len(shape))
    per_expert = lambda *shape: pl.BlockSpec((per,) + shape, lambda x, p: (x, 0, 0))
    block_f = width // n_dp
    partial, hot, gate_col = pl.pallas_call(
        functools.partial(weight_kernel, dims=dims),
        out_shape=(
            jax.ShapeDtypeStruct((n_dp, experts, block_f, block), BF),
            jax.ShapeDtypeStruct((n_expert, experts * half, tokens), BF),
            jax.ShapeDtypeStruct((experts * half, 128), F32),
        ),
        grid_spec=pltpu.PrefetchScalarGridSpec(
            num_scalar_prefetch=1,
            grid=(experts // per,),
            in_specs=[whole(*tok.shape), whole(*meta.shape), per_expert(slots, width)],
            out_specs=(
                pl.BlockSpec((n_dp, per, block_f, block), lambda x, p: (0, x, 0, 0)),
                whole(n_expert, experts * half, tokens),
                whole(experts * half, 128),
            ),
            scratch_shapes=[pltpu.VMEM((experts, slots, block), BF)],
        ),
        compiler_params=params,
        cost_estimate=cost,
        name="weight_part",
    )(place, tok, meta, hidden_saved[0])
    total = lax.psum_scatter(partial, "dp", scatter_dimension=0, tiled=True)[0]

    pairs, near_steps = chips // 2, experts // per // 2
    out_block = (pairs, per, half, width)
    keep, near, far = pl.pallas_call(
        part_kernel,
        out_shape=(
            jax.ShapeDtypeStruct((pairs, experts, half, width), BF),
            jax.ShapeDtypeStruct((pairs, experts // 2, half, width), BF),
            jax.ShapeDtypeStruct((pairs, experts // 2, half, width), BF),
        ),
        grid_spec=pltpu.PrefetchScalarGridSpec(
            num_scalar_prefetch=1,
            grid=(experts // per,),
            in_specs=[
                whole(*tok.shape),
                whole(*tok.shape),
                whole(*hot.shape),
                per_expert(width, block),
                per_expert(width, block),
            ],
            out_specs=(
                pl.BlockSpec(out_block, lambda x, p: (0, x, 0, 0)),
                pl.BlockSpec(out_block, lambda x, p: (0, jnp.minimum(x, near_steps - 1), 0, 0)),
                pl.BlockSpec(out_block, lambda x, p: (0, jnp.maximum(x - near_steps, 0), 0, 0)),
            ),
            scratch_shapes=[pltpu.VMEM((experts, slots // 2, block), F32)] * 2,
        ),
        compiler_params=params,
        cost_estimate=cost,
        name="hidden_part",
    )(place, tok, other, hot, w_down, w_other)

    def swap(shift):
        at = lambda z: (z ^ 1) if shift == 0 else ((((z + 1) % chips) ^ 1) - 1) % chips
        return [(2 * z + c, 2 * at(z) + c) for z in range(chips) for c in range(2)]

    near = lax.ppermute(near, "tensor", swap(0))
    far = lax.ppermute(far, "tensor", swap(1))
    row = lambda n: pl.BlockSpec((1, n, half, width), lambda m: (m, 0, 0, 0))
    parts = pl.pallas_call(
        add_kernel,
        out_shape=jax.ShapeDtypeStruct(keep.shape, BF),
        grid=(pairs,),
        in_specs=[row(experts), row(experts // 2), row(experts // 2)],
        out_specs=row(experts),
        compiler_params=params,
        name="pair_sum",
    )(keep, near, far)
    same_kind = [
        [2 * (2 * m + p) + c for m in range(pairs)] for p in range(2) for c in range(2)
    ]
    parts = lax.all_to_all(parts, "tensor", 0, 0, tiled=True, axis_index_groups=same_kind)
    grad_hidden, grad_gates = pl.pallas_call(
        finish_kernel,
        out_shape=(
            jax.ShapeDtypeStruct((experts, half, width), BF),
            jax.ShapeDtypeStruct((experts, half), F32),
        ),
        in_specs=[pl.BlockSpec(memory_space=pltpu.VMEM)] * 3,
        out_specs=(pl.BlockSpec(memory_space=pltpu.VMEM),) * 2,
        compiler_params=pltpu.CompilerParams(vmem_limit_bytes=32 * 1024 * 1024),
        name="finish",
    )(parts, gate_col, my_hidden)
    return grad_hidden[None], grad_gates[None], total


def solution(mesh):
    in_specs = (
        P("dp", "expert", "tensor", None),
        P("dp", "expert", None, None),
        P("dp", "expert", None, None),
        P("dp", "expert", None, None),
        P("expert", None, "tensor"),
    )
    out_specs = (
        P("dp", "expert", "tensor", None),
        P("dp", "expert", "tensor"),
        P("expert", "dp", "tensor"),
    )
    return jax.shard_map(local, mesh=mesh, in_specs=in_specs, out_specs=out_specs, check_vma=False)
```

```python
import functools

import jax
import jax.numpy as jnp
from jax import lax
from jax.experimental import pallas as pl
from jax.experimental.pallas import tpu as pltpu
from jax.sharding import PartitionSpec as P

BF = jnp.bfloat16
F32 = jnp.float32


def iota(shape, dim):
    return lax.broadcasted_iota(jnp.int32, shape, dim)


def tables(meta_ref, columns, first, experts, tokens, choices):
    expert_of = (first + iota((experts, tokens), 0)).astype(F32)
    named, gates = [], []
    for c in range(columns):
        meta = meta_ref[c].astype(F32)
        hit_any = jnp.zeros((experts, tokens), F32)
        gate = jnp.zeros((experts, tokens), F32)
        for k in range(choices):
            hit = meta[k : k + 1, :] == expert_of
            hit_any = jnp.where(hit, 1.0, hit_any)
            gate = jnp.where(hit, meta[choices + k : choices + k + 1, :], gate)
        named.append(hit_any)
        gates.append(gate)
    named = jnp.concatenate(named, 0)
    before = (iota((tokens, tokens), 0) < iota((tokens, tokens), 1)).astype(F32).astype(BF)
    rank = jnp.dot(named.astype(BF), before, preferred_element_type=F32)
    table = jnp.where(named > 0, rank, -1.0)
    return [table[c * experts : (c + 1) * experts] for c in range(columns)], gates


def picker(table, gate, base, slots, experts, tokens):
    rank = (base + iota((slots, tokens), 0)).astype(F32)
    rows = []
    for x in range(experts):
        value = 1.0 if gate is None else gate[x : x + 1, :]
        rows.append(jnp.where(table[x : x + 1, :] == rank, value, 0.0))
    return jnp.concatenate(rows, 0)


def pick_kernel(place, meta_ref, scaled_hot_ref, hot_ref, gate_ref, *, dims):
    experts, columns, tokens, choices, most = dims
    half = most // 2
    base = place[2] * half
    table, gates = tables(meta_ref, columns, place[0] * experts, experts, tokens, choices)
    for c in range(columns):
        scaled_hot_ref[c] = picker(table[c], gates[c], 0, most, experts, tokens).astype(BF)
        hot_ref[c] = picker(table[c], None, base, half, experts, tokens).astype(BF)

        @pl.when(place[1] == c)
        def _():
            gate = picker(table[c], gates[c], base, half, experts, tokens)
            gate_ref[...] = jnp.broadcast_to(jnp.sum(gate, axis=1, keepdims=True), gate_ref.shape)


def weight_kernel(tok_ref, hot_ref, hidden_ref, out_ref, scaled):
    experts = scaled.shape[0]
    columns = tok_ref.shape[0]
    most = scaled.shape[1] // columns
    step = pl.program_id(0)
    per = hidden_ref.shape[0]

    @pl.when(step == 0)
    def _():
        for c in range(columns):
            rows = jnp.dot(hot_ref[c], tok_ref[c], preferred_element_type=F32).astype(BF)
            for x in range(experts):
                scaled[x, c * most : (c + 1) * most, :] = rows[x * most : (x + 1) * most]

    for i in range(per):
        part = lax.dot_general(
            hidden_ref[i],
            scaled[step * per + i],
            (((0,), (0,)), ((), ())),
            preferred_element_type=F32,
        )
        n_dp, _, block_f, block = out_ref.shape
        out_ref[:, i] = part.astype(BF).reshape(n_dp, block_f, block)


def part_kernel(
    place, tok_ref, other_ref, hot_ref, w_ref, w_other_ref, keep_ref, near_ref, far_ref, mine, theirs
):
    columns, rows_half, _ = hot_ref.shape
    experts = mine.shape[0]
    half = rows_half // experts
    step = pl.program_id(0)
    per = w_ref.shape[0]

    @pl.when(step == 0)
    def _():
        for c in range(columns):
            for src, dst in ((tok_ref, mine), (other_ref, theirs)):
                rows = jnp.dot(hot_ref[c], src[c], preferred_element_type=F32)
                for x in range(experts):
                    dst[x, c * half : (c + 1) * half, :] = rows[x * half : (x + 1) * half]

    dims_nt = (((1,), (1,)), ((), ()))
    odd = place[1] % 2 == 1
    for i in range(per):
        x = step * per + i
        part = lax.dot_general(mine[x].astype(BF), w_ref[i], dims_nt, preferred_element_type=F32)
        part = part + lax.dot_general(
            theirs[x].astype(BF), w_other_ref[i], dims_nt, preferred_element_type=F32
        )
        part = part.reshape(columns // 2, 2, half, part.shape[1])
        keep_ref[:, i] = jnp.where(odd, part[:, 1], part[:, 0]).astype(BF)
        give = jnp.where(odd, part[:, 0], part[:, 1]).astype(BF)

        @pl.when(x < experts // 2)
        def _():
            near_ref[:, i] = give

        @pl.when(x >= experts // 2)
        def _():
            far_ref[:, i] = give


def add_kernel(keep_ref, near_ref, far_ref, out_ref):
    h = near_ref.shape[1]
    out_ref[:, :h] = (keep_ref[:, :h].astype(F32) + near_ref[...].astype(F32)).astype(BF)
    out_ref[:, h:] = (keep_ref[:, h:].astype(F32) + far_ref[...].astype(F32)).astype(BF)


def finish_kernel(parts_ref, gate_ref, hidden_ref, grad_ref, gates_ref):
    sources, experts, half, width = parts_ref.shape
    values = parts_ref[0].astype(F32)
    for s in range(1, sources):
        values = values + parts_ref[s].astype(F32)
    gate = gate_ref[:, :1].reshape(experts, half, 1)
    grad_ref[...] = (gate * values).astype(BF)
    gates_ref[...] = jnp.sum(hidden_ref[...].astype(F32) * values, axis=2)


def local(grad_out, routes, gates, hidden_saved, w_down):
    n_tensor = lax.axis_size("tensor")
    n_expert = lax.axis_size("expert")
    n_dp = lax.axis_size("dp")
    chips = n_tensor // 2
    experts, width, block = w_down.shape
    slots = hidden_saved.shape[2]
    most = slots // n_expert
    half = most // 2
    tokens, choices = routes.shape[2:]
    own = grad_out.shape[2]
    dims = (experts, n_expert, tokens, choices, most)
    me = lax.axis_index("tensor")
    place = jnp.stack([lax.axis_index("expert"), me // 2, me % 2]).astype(jnp.int32)
    pair = [(i, i ^ 1) for i in range(n_tensor)]
    params = pltpu.CompilerParams(vmem_limit_bytes=50 * 1024 * 1024)

    work = 2 * experts * slots * width * block + 2 * n_expert * slots * tokens * block
    cost = pl.CostEstimate(flops=work, bytes_accessed=2 * w_down.size, transcendentals=0)

    w_other = lax.ppermute(w_down, "tensor", pair)
    first = me * (slots // n_tensor)
    my_hidden = lax.dynamic_slice_in_dim(hidden_saved[0], first, slots // n_tensor, 1)

    meta = jnp.concatenate([routes[0, 0].T.astype(BF), gates[0, 0].T], 0)
    meta = jnp.broadcast_to(meta[None], (n_expert,) + meta.shape)
    meta = lax.all_to_all(meta, "expert", 0, 0, tiled=True)
    whole = lambda *shape: pl.BlockSpec(shape, lambda x, p: (0,) * len(shape))
    scaled_hot, hot, gate_col = pl.pallas_call(
        functools.partial(pick_kernel, dims=dims),
        out_shape=(
            jax.ShapeDtypeStruct((n_expert, experts * most, tokens), BF),
            jax.ShapeDtypeStruct((n_expert, experts * half, tokens), BF),
            jax.ShapeDtypeStruct((experts * half, 128), F32),
        ),
        grid_spec=pltpu.PrefetchScalarGridSpec(
            num_scalar_prefetch=1,
            grid=(1,),
            in_specs=[whole(*meta.shape)],
            out_specs=(
                whole(n_expert, experts * most, tokens),
                whole(n_expert, experts * half, tokens),
                whole(experts * half, 128),
            ),
        ),
        compiler_params=params,
        cost_estimate=cost,
        name="pick",
    )(place, meta)
    scaled_hot, w_other = lax.optimization_barrier((scaled_hot, w_other))
    send = grad_out[0, 0].reshape(own, n_tensor, block).transpose(1, 0, 2)
    send = jnp.broadcast_to(send[None], (n_expert,) + send.shape)
    send = send.reshape(n_expert * n_tensor, own, block)
    send, _ = lax.optimization_barrier((send, meta))
    tok = lax.all_to_all(send, ("expert", "tensor"), 0, 0, tiled=True)
    tok = tok.reshape(n_expert, tokens, block)
    other = lax.ppermute(tok, "tensor", pair)

    per = 2
    whole = lambda *shape: pl.BlockSpec(shape, lambda x: (0,) * len(shape))
    per_expert = lambda *shape: pl.BlockSpec((per,) + shape, lambda x: (x, 0, 0))
    block_f = width // n_dp
    partial = pl.pallas_call(
        weight_kernel,
        out_shape=jax.ShapeDtypeStruct((n_dp, experts, block_f, block), BF),
        grid=(experts // per,),
        in_specs=[whole(*tok.shape), whole(*scaled_hot.shape), per_expert(slots, width)],
        out_specs=pl.BlockSpec((n_dp, per, block_f, block), lambda x: (0, x, 0, 0)),
        scratch_shapes=[pltpu.VMEM((experts, slots, block), BF)],
        compiler_params=params,
        cost_estimate=cost,
        name="weight_part",
    )(tok, scaled_hot, hidden_saved[0])
    total = lax.psum_scatter(partial, "dp", scatter_dimension=0, tiled=True)[0]

    pairs, near_steps = chips // 2, experts // per // 2
    out_block = (pairs, per, half, width)
    whole_p = lambda *shape: pl.BlockSpec(shape, lambda x, p: (0,) * len(shape))
    per_expert_p = lambda *shape: pl.BlockSpec((per,) + shape, lambda x, p: (x, 0, 0))
    keep, near, far = pl.pallas_call(
        part_kernel,
        out_shape=(
            jax.ShapeDtypeStruct((pairs, experts, half, width), BF),
            jax.ShapeDtypeStruct((pairs, experts // 2, half, width), BF),
            jax.ShapeDtypeStruct((pairs, experts // 2, half, width), BF),
        ),
        grid_spec=pltpu.PrefetchScalarGridSpec(
            num_scalar_prefetch=1,
            grid=(experts // per,),
            in_specs=[
                whole_p(*tok.shape),
                whole_p(*tok.shape),
                whole_p(*hot.shape),
                per_expert_p(width, block),
                per_expert_p(width, block),
            ],
            out_specs=(
                pl.BlockSpec(out_block, lambda x, p: (0, x, 0, 0)),
                pl.BlockSpec(out_block, lambda x, p: (0, jnp.minimum(x, near_steps - 1), 0, 0)),
                pl.BlockSpec(out_block, lambda x, p: (0, jnp.maximum(x - near_steps, 0), 0, 0)),
            ),
            scratch_shapes=[pltpu.VMEM((experts, slots // 2, block), F32)] * 2,
        ),
        compiler_params=params,
        cost_estimate=cost,
        name="hidden_part",
    )(place, tok, other, hot, w_down, w_other)

    def swap(shift):
        at = lambda z: (z ^ 1) if shift == 0 else ((((z + 1) % chips) ^ 1) - 1) % chips
        return [(2 * z + c, 2 * at(z) + c) for z in range(chips) for c in range(2)]

    near = lax.ppermute(near, "tensor", swap(0))
    far = lax.ppermute(far, "tensor", swap(1))
    row = lambda n: pl.BlockSpec((1, n, half, width), lambda m: (m, 0, 0, 0))
    parts = pl.pallas_call(
        add_kernel,
        out_shape=jax.ShapeDtypeStruct(keep.shape, BF),
        grid=(pairs,),
        in_specs=[row(experts), row(experts // 2), row(experts // 2)],
        out_specs=row(experts),
        compiler_params=params,
        name="pair_sum",
    )(keep, near, far)
    same_kind = [
        [2 * (2 * m + p) + c for m in range(pairs)] for p in range(2) for c in range(2)
    ]
    parts = lax.all_to_all(parts, "tensor", 0, 0, tiled=True, axis_index_groups=same_kind)
    grad_hidden, grad_gates = pl.pallas_call(
        finish_kernel,
        out_shape=(
            jax.ShapeDtypeStruct((experts, half, width), BF),
            jax.ShapeDtypeStruct((experts, half), F32),
        ),
        in_specs=[pl.BlockSpec(memory_space=pltpu.VMEM)] * 3,
        out_specs=(pl.BlockSpec(memory_space=pltpu.VMEM),) * 2,
        compiler_params=pltpu.CompilerParams(vmem_limit_bytes=32 * 1024 * 1024),
        name="finish",
    )(parts, gate_col, my_hidden)
    return grad_hidden[None], grad_gates[None], total


def solution(mesh):
    in_specs = (
        P("dp", "expert", "tensor", None),
        P("dp", "expert", None, None),
        P("dp", "expert", None, None),
        P("dp", "expert", None, None),
        P("expert", None, "tensor"),
    )
    out_specs = (
        P("dp", "expert", "tensor", None),
        P("dp", "expert", "tensor"),
        P("expert", "dp", "tensor"),
    )
    return jax.shard_map(local, mesh=mesh, in_specs=in_specs, out_specs=out_specs, check_vma=False)
```

```python
import functools

import jax
import jax.numpy as jnp
from jax import lax
from jax.experimental import pallas as pl
from jax.experimental.pallas import tpu as pltpu
from jax.sharding import PartitionSpec as P

BF = jnp.bfloat16
F32 = jnp.float32


def iota(shape, dim):
    return lax.broadcasted_iota(jnp.int32, shape, dim)


def tables(meta_ref, columns, first, experts, tokens, choices):
    expert_of = (first + iota((experts, tokens), 0)).astype(F32)
    named, gates = [], []
    for c in range(columns):
        meta = meta_ref[c, tokens:, :].astype(F32)
        hit_any = jnp.zeros((experts, tokens), F32)
        gate = jnp.zeros((experts, tokens), F32)
        for k in range(choices):
            hit = meta[k : k + 1, :] == expert_of
            hit_any = jnp.where(hit, 1.0, hit_any)
            gate = jnp.where(hit, meta[choices + k : choices + k + 1, :], gate)
        named.append(hit_any)
        gates.append(gate)
    named = jnp.concatenate(named, 0)
    before = (iota((tokens, tokens), 0) < iota((tokens, tokens), 1)).astype(F32).astype(BF)
    rank = jnp.dot(named.astype(BF), before, preferred_element_type=F32)
    table = jnp.where(named > 0, rank, -1.0)
    return [table[c * experts : (c + 1) * experts] for c in range(columns)], gates


def picker(table, gate, base, slots, experts, tokens):
    rank = (base + iota((slots, tokens), 0)).astype(F32)
    rows = []
    for x in range(experts):
        value = 1.0 if gate is None else gate[x : x + 1, :]
        rows.append(jnp.where(table[x : x + 1, :] == rank, value, 0.0))
    return jnp.concatenate(rows, 0)


def pick_kernel(place, meta_ref, scaled_hot_ref, hot_ref, gate_ref, *, dims):
    experts, columns, tokens, choices, most = dims
    half = most // 2
    base = place[2] * half
    table, gates = tables(meta_ref, columns, place[0] * experts, experts, tokens, choices)
    for c in range(columns):
        scaled_hot_ref[c] = picker(table[c], gates[c], 0, most, experts, tokens).astype(BF)
        hot_ref[c] = picker(table[c], None, base, half, experts, tokens).astype(BF)

        @pl.when(place[1] == c)
        def _():
            gate = picker(table[c], gates[c], base, half, experts, tokens)
            gate_ref[...] = jnp.broadcast_to(jnp.sum(gate, axis=1, keepdims=True), gate_ref.shape)


def weight_kernel(tok_ref, hot_ref, hidden_ref, out_ref, scaled):
    experts = scaled.shape[0]
    columns = tok_ref.shape[0]
    most = scaled.shape[1] // columns
    step = pl.program_id(0)
    per = hidden_ref.shape[0]

    @pl.when(step == 0)
    def _():
        for c in range(columns):
            rows = jnp.dot(hot_ref[c], tok_ref[c, : hot_ref.shape[2]], preferred_element_type=F32)
            rows = rows.astype(BF)
            for x in range(experts):
                scaled[x, c * most : (c + 1) * most, :] = rows[x * most : (x + 1) * most]

    for i in range(per):
        part = lax.dot_general(
            hidden_ref[i],
            scaled[step * per + i],
            (((0,), (0,)), ((), ())),
            preferred_element_type=F32,
        )
        n_dp, _, block_f, block = out_ref.shape
        out_ref[:, i] = part.astype(BF).reshape(n_dp, block_f, block)


def part_kernel(
    place, tok_ref, other_ref, hot_ref, w_ref, w_other_ref, keep_ref, near_ref, far_ref, mine, theirs
):
    columns, rows_half, _ = hot_ref.shape
    experts = mine.shape[0]
    half = rows_half // experts
    step = pl.program_id(0)
    per = w_ref.shape[0]

    @pl.when(step == 0)
    def _():
        for c in range(columns):
            for src, dst in ((tok_ref, mine), (other_ref, theirs)):
                rows = jnp.dot(
                    hot_ref[c], src[c, : hot_ref.shape[2]], preferred_element_type=F32
                )
                for x in range(experts):
                    dst[x, c * half : (c + 1) * half, :] = rows[x * half : (x + 1) * half]

    dims_nt = (((1,), (1,)), ((), ()))
    odd = place[1] % 2 == 1
    for i in range(per):
        x = step * per + i
        part = lax.dot_general(mine[x].astype(BF), w_ref[i], dims_nt, preferred_element_type=F32)
        part = part + lax.dot_general(
            theirs[x].astype(BF), w_other_ref[i], dims_nt, preferred_element_type=F32
        )
        part = part.reshape(columns // 2, 2, half, part.shape[1])
        keep_ref[:, i] = jnp.where(odd, part[:, 1], part[:, 0]).astype(BF)
        give = jnp.where(odd, part[:, 0], part[:, 1]).astype(BF)

        @pl.when(x < experts // 2)
        def _():
            near_ref[:, i] = give

        @pl.when(x >= experts // 2)
        def _():
            far_ref[:, i] = give


def add_kernel(keep_ref, near_ref, far_ref, out_ref):
    h = near_ref.shape[1]
    out_ref[:, :h] = (keep_ref[:, :h].astype(F32) + near_ref[...].astype(F32)).astype(BF)
    out_ref[:, h:] = (keep_ref[:, h:].astype(F32) + far_ref[...].astype(F32)).astype(BF)


def finish_kernel(parts_ref, gate_ref, hidden_ref, grad_ref, gates_ref):
    sources, experts, half, width = parts_ref.shape
    values = parts_ref[0].astype(F32)
    for s in range(1, sources):
        values = values + parts_ref[s].astype(F32)
    gate = gate_ref[:, :1].reshape(experts, half, 1)
    grad_ref[...] = (gate * values).astype(BF)
    gates_ref[...] = jnp.sum(hidden_ref[...].astype(F32) * values, axis=2)


def local(grad_out, routes, gates, hidden_saved, w_down):
    n_tensor = lax.axis_size("tensor")
    n_expert = lax.axis_size("expert")
    n_dp = lax.axis_size("dp")
    chips = n_tensor // 2
    experts, width, block = w_down.shape
    slots = hidden_saved.shape[2]
    most = slots // n_expert
    half = most // 2
    tokens, choices = routes.shape[2:]
    own = grad_out.shape[2]
    dims = (experts, n_expert, tokens, choices, most)
    me = lax.axis_index("tensor")
    place = jnp.stack([lax.axis_index("expert"), me // 2, me % 2]).astype(jnp.int32)
    pair = [(i, i ^ 1) for i in range(n_tensor)]
    params = pltpu.CompilerParams(vmem_limit_bytes=50 * 1024 * 1024)

    work = 2 * experts * slots * width * block + 2 * n_expert * slots * tokens * block
    cost = pl.CostEstimate(flops=work, bytes_accessed=2 * w_down.size, transcendentals=0)

    w_other = lax.ppermute(w_down, "tensor", pair)
    first = me * (slots // n_tensor)
    my_hidden = lax.dynamic_slice_in_dim(hidden_saved[0], first, slots // n_tensor, 1)

    send = grad_out[0, 0].reshape(own, n_tensor, block).transpose(1, 0, 2)
    column = lax.all_to_all(send, "tensor", 0, 0, tiled=True).reshape(tokens, block)
    packed = jnp.concatenate([column, routes[0, 0].T.astype(BF), gates[0, 0].T], 0)
    packed = jnp.broadcast_to(packed[None], (n_expert,) + packed.shape)
    tok = lax.all_to_all(packed, "expert", 0, 0, tiled=True)
    vmem = pl.BlockSpec(memory_space=pltpu.VMEM)
    scaled_hot, hot, gate_col = pl.pallas_call(
        functools.partial(pick_kernel, dims=dims),
        out_shape=(
            jax.ShapeDtypeStruct((n_expert, experts * most, tokens), BF),
            jax.ShapeDtypeStruct((n_expert, experts * half, tokens), BF),
            jax.ShapeDtypeStruct((experts * half, 128), F32),
        ),
        grid_spec=pltpu.PrefetchScalarGridSpec(
            num_scalar_prefetch=1,
            grid=(1,),
            in_specs=[vmem],
            out_specs=(
                vmem,
                vmem,
                vmem,
            ),
        ),
        compiler_params=params,
        cost_estimate=cost,
        name="pick",
    )(place, tok)
    tok, w_other = lax.optimization_barrier((tok, w_other))
    other = lax.ppermute(tok, "tensor", pair)

    per = 2
    per_expert = lambda *shape: pl.BlockSpec((per,) + shape, lambda x: (x, 0, 0))
    block_f = width // n_dp
    pairs, near_steps = chips // 2, experts // per // 2
    out_block = (pairs, per, half, width)
    per_expert_p = lambda *shape: pl.BlockSpec((per,) + shape, lambda x, p: (x, 0, 0))
    keep, near, far = pl.pallas_call(
        part_kernel,
        out_shape=(
            jax.ShapeDtypeStruct((pairs, experts, half, width), BF),
            jax.ShapeDtypeStruct((pairs, experts // 2, half, width), BF),
            jax.ShapeDtypeStruct((pairs, experts // 2, half, width), BF),
        ),
        grid_spec=pltpu.PrefetchScalarGridSpec(
            num_scalar_prefetch=1,
            grid=(experts // per,),
            in_specs=[
                vmem,
                vmem,
                vmem,
                per_expert_p(width, block),
                per_expert_p(width, block),
            ],
            out_specs=(
                pl.BlockSpec(out_block, lambda x, p: (0, x, 0, 0)),
                pl.BlockSpec(out_block, lambda x, p: (0, jnp.minimum(x, near_steps - 1), 0, 0)),
                pl.BlockSpec(out_block, lambda x, p: (0, jnp.maximum(x - near_steps, 0), 0, 0)),
            ),
            scratch_shapes=[pltpu.VMEM((experts, slots // 2, block), F32)] * 2,
        ),
        compiler_params=params,
        cost_estimate=cost,
        name="hidden_part",
    )(place, tok, other, hot, w_down, w_other)

    most_per = 4
    scaled_hot, _ = lax.optimization_barrier((scaled_hot, keep))
    partial = pl.pallas_call(
        weight_kernel,
        out_shape=jax.ShapeDtypeStruct((n_dp, experts, block_f, block), BF),
        grid=(experts // most_per,),
        in_specs=[vmem, vmem, pl.BlockSpec((most_per, slots, width), lambda x: (x, 0, 0))],
        out_specs=pl.BlockSpec((n_dp, most_per, block_f, block), lambda x: (0, x, 0, 0)),
        scratch_shapes=[pltpu.VMEM((experts, slots, block), BF)],
        compiler_params=params,
        cost_estimate=cost,
        name="weight_part",
    )(tok, scaled_hot, hidden_saved[0])
    total = lax.psum_scatter(partial, "dp", scatter_dimension=0, tiled=True)[0]

    def swap(shift):
        at = lambda z: (z ^ 1) if shift == 0 else ((((z + 1) % chips) ^ 1) - 1) % chips
        return [(2 * z + c, 2 * at(z) + c) for z in range(chips) for c in range(2)]

    near = lax.ppermute(near, "tensor", swap(0))
    far = lax.ppermute(far, "tensor", swap(1))
    row = lambda n: pl.BlockSpec((1, n, half, width), lambda m: (m, 0, 0, 0))
    parts = pl.pallas_call(
        add_kernel,
        out_shape=jax.ShapeDtypeStruct(keep.shape, BF),
        grid=(pairs,),
        in_specs=[row(experts), row(experts // 2), row(experts // 2)],
        out_specs=row(experts),
        compiler_params=params,
        name="pair_sum",
    )(keep, near, far)
    same_kind = [
        [2 * (2 * m + p) + c for m in range(pairs)] for p in range(2) for c in range(2)
    ]
    parts = lax.all_to_all(parts, "tensor", 0, 0, tiled=True, axis_index_groups=same_kind)
    grad_hidden, grad_gates = pl.pallas_call(
        finish_kernel,
        out_shape=(
            jax.ShapeDtypeStruct((experts, half, width), BF),
            jax.ShapeDtypeStruct((experts, half), F32),
        ),
        in_specs=[pl.BlockSpec(memory_space=pltpu.VMEM)] * 3,
        out_specs=(pl.BlockSpec(memory_space=pltpu.VMEM),) * 2,
        compiler_params=pltpu.CompilerParams(vmem_limit_bytes=32 * 1024 * 1024),
        name="finish",
    )(parts, gate_col, my_hidden)
    return grad_hidden[None], grad_gates[None], total


def solution(mesh):
    in_specs = (
        P("dp", "expert", "tensor", None),
        P("dp", "expert", None, None),
        P("dp", "expert", None, None),
        P("dp", "expert", None, None),
        P("expert", None, "tensor"),
    )
    out_specs = (
        P("dp", "expert", "tensor", None),
        P("dp", "expert", "tensor"),
        P("expert", "dp", "tensor"),
    )
    return jax.shard_map(local, mesh=mesh, in_specs=in_specs, out_specs=out_specs, check_vma=False)
```

```python
import functools

import jax
import jax.numpy as jnp
from jax import lax
from jax.experimental import pallas as pl
from jax.experimental.pallas import tpu as pltpu
from jax.sharding import PartitionSpec as P

BF = jnp.bfloat16
F32 = jnp.float32


def iota(shape, dim):
    return lax.broadcasted_iota(jnp.int32, shape, dim)


def tables(meta_ref, columns, first, experts, tokens, choices):
    expert_of = (first + iota((experts, tokens), 0)).astype(F32)
    named, gates = [], []
    for c in range(columns):
        meta = meta_ref[c, tokens:, :].astype(F32)
        hit_any = jnp.zeros((experts, tokens), F32)
        gate = jnp.zeros((experts, tokens), F32)
        for k in range(choices):
            hit = meta[k : k + 1, :] == expert_of
            hit_any = jnp.where(hit, 1.0, hit_any)
            gate = jnp.where(hit, meta[choices + k : choices + k + 1, :], gate)
        named.append(hit_any)
        gates.append(gate)
    named = jnp.concatenate(named, 0)
    before = (iota((tokens, tokens), 0) < iota((tokens, tokens), 1)).astype(F32).astype(BF)
    rank = jnp.dot(named.astype(BF), before, preferred_element_type=F32)
    table = jnp.where(named > 0, rank, -1.0)
    return [table[c * experts : (c + 1) * experts] for c in range(columns)], gates


def picker(table, gate, base, slots, experts, tokens):
    rank = (base + iota((slots, tokens), 0)).astype(F32)
    rows = []
    for x in range(experts):
        value = 1.0 if gate is None else gate[x : x + 1, :]
        rows.append(jnp.where(table[x : x + 1, :] == rank, value, 0.0))
    return jnp.concatenate(rows, 0)


def pick_kernel(place, meta_ref, scaled_hot_ref, hot_ref, gate_ref, *, dims):
    experts, columns, tokens, choices, most = dims
    half = most // 2
    base = place[2] * half
    table, gates = tables(meta_ref, columns, place[0] * experts, experts, tokens, choices)
    for c in range(columns):
        scaled_hot_ref[c] = picker(table[c], gates[c], 0, most, experts, tokens).astype(BF)
        hot_ref[c] = picker(table[c], None, base, half, experts, tokens).astype(BF)

        @pl.when(place[1] == c)
        def _():
            gate = picker(table[c], gates[c], base, half, experts, tokens)
            gate_ref[...] = jnp.broadcast_to(jnp.sum(gate, axis=1, keepdims=True), gate_ref.shape)


def weight_kernel(tok_ref, hot_ref, hidden_ref, out_ref, scaled):
    experts = scaled.shape[0]
    columns = tok_ref.shape[0]
    most = scaled.shape[1] // columns
    step = pl.program_id(0)
    per = hidden_ref.shape[0]

    @pl.when(step == 0)
    def _():
        for c in range(columns):
            rows = jnp.dot(hot_ref[c], tok_ref[c, : hot_ref.shape[2]], preferred_element_type=F32)
            rows = rows.astype(BF)
            for x in range(experts):
                scaled[x, c * most : (c + 1) * most, :] = rows[x * most : (x + 1) * most]

    for i in range(per):
        part = lax.dot_general(
            hidden_ref[i],
            scaled[step * per + i],
            (((0,), (0,)), ((), ())),
            preferred_element_type=F32,
        )
        n_dp, _, block_f, block = out_ref.shape
        out_ref[:, i] = part.astype(BF).reshape(n_dp, block_f, block)


def part_kernel(
    place, tok_ref, other_ref, hot_ref, w_ref, w_other_ref, keep_ref, near_ref, far_ref, mine, theirs
):
    columns, rows_half, _ = hot_ref.shape
    experts = mine.shape[0]
    half = rows_half // experts
    step = pl.program_id(0)
    per = w_ref.shape[0]

    @pl.when(step == 0)
    def _():
        for c in range(columns):
            for src, dst in ((tok_ref, mine), (other_ref, theirs)):
                rows = jnp.dot(
                    hot_ref[c], src[c, : hot_ref.shape[2]], preferred_element_type=F32
                )
                for x in range(experts):
                    dst[x, c * half : (c + 1) * half, :] = rows[x * half : (x + 1) * half]

    dims_nt = (((1,), (1,)), ((), ()))
    odd = place[1] % 2 == 1
    for i in range(per):
        x = step * per + i
        part = lax.dot_general(mine[x].astype(BF), w_ref[i], dims_nt, preferred_element_type=F32)
        part = part + lax.dot_general(
            theirs[x].astype(BF), w_other_ref[i], dims_nt, preferred_element_type=F32
        )
        part = part.reshape(columns // 2, 2, half, part.shape[1])
        keep_ref[:, i] = jnp.where(odd, part[:, 1], part[:, 0]).astype(BF)
        give = jnp.where(odd, part[:, 0], part[:, 1]).astype(BF)

        @pl.when(x < experts // 2)
        def _():
            near_ref[:, i] = give

        @pl.when(x >= experts // 2)
        def _():
            far_ref[:, i] = give


def add_kernel(keep_ref, near_ref, far_ref, out_ref):
    h = near_ref.shape[1]
    out_ref[:, :h] = (keep_ref[:, :h].astype(F32) + near_ref[...].astype(F32)).astype(BF)
    out_ref[:, h:] = (keep_ref[:, h:].astype(F32) + far_ref[...].astype(F32)).astype(BF)


def finish_kernel(parts_ref, gate_ref, hidden_ref, grad_ref, gates_ref):
    sources, experts, half, width = parts_ref.shape
    values = parts_ref[0].astype(F32)
    for s in range(1, sources):
        values = values + parts_ref[s].astype(F32)
    gate = gate_ref[:, :1].reshape(experts, half, 1)
    grad_ref[...] = (gate * values).astype(BF)
    gates_ref[...] = jnp.sum(hidden_ref[...].astype(F32) * values, axis=2)


def local(grad_out, routes, gates, hidden_saved, w_down):
    n_tensor = lax.axis_size("tensor")
    n_expert = lax.axis_size("expert")
    n_dp = lax.axis_size("dp")
    chips = n_tensor // 2
    experts, width, block = w_down.shape
    slots = hidden_saved.shape[2]
    most = slots // n_expert
    half = most // 2
    tokens, choices = routes.shape[2:]
    own = grad_out.shape[2]
    dims = (experts, n_expert, tokens, choices, most)
    me = lax.axis_index("tensor")
    place = jnp.stack([lax.axis_index("expert"), me // 2, me % 2]).astype(jnp.int32)
    pair = [(i, i ^ 1) for i in range(n_tensor)]
    params = pltpu.CompilerParams(vmem_limit_bytes=50 * 1024 * 1024)

    work = 2 * experts * slots * width * block + 2 * n_expert * slots * tokens * block
    cost = pl.CostEstimate(flops=work, bytes_accessed=2 * w_down.size, transcendentals=0)

    w_other = lax.ppermute(w_down, "tensor", pair)
    first = me * (slots // n_tensor)
    my_hidden = lax.dynamic_slice_in_dim(hidden_saved[0], first, slots // n_tensor, 1)

    send = grad_out[0, 0].reshape(own, n_tensor, block).transpose(1, 0, 2)
    column = lax.all_to_all(send, "tensor", 0, 0, tiled=True).reshape(tokens, block)
    packed = jnp.concatenate([column, routes[0, 0].T.astype(BF), gates[0, 0].T], 0)
    packed = jnp.broadcast_to(packed[None], (n_expert,) + packed.shape)
    tok = lax.all_to_all(packed, "expert", 0, 0, tiled=True)
    vmem = pl.BlockSpec(memory_space=pltpu.VMEM)
    scaled_hot, hot, gate_col = pl.pallas_call(
        functools.partial(pick_kernel, dims=dims),
        out_shape=(
            jax.ShapeDtypeStruct((n_expert, experts * most, tokens), BF),
            jax.ShapeDtypeStruct((n_expert, experts * half, tokens), BF),
            jax.ShapeDtypeStruct((experts * half, 128), F32),
        ),
        grid_spec=pltpu.PrefetchScalarGridSpec(
            num_scalar_prefetch=1,
            grid=(1,),
            in_specs=[vmem],
            out_specs=(
                vmem,
                vmem,
                vmem,
            ),
        ),
        compiler_params=params,
        cost_estimate=cost,
        name="pick",
    )(place, tok)
    other = lax.ppermute(tok, "tensor", pair)

    per = 2
    per_expert = lambda *shape: pl.BlockSpec((per,) + shape, lambda x: (x, 0, 0))
    block_f = width // n_dp
    pairs, near_steps = chips // 2, experts // per // 2
    out_block = (pairs, per, half, width)
    per_expert_p = lambda *shape: pl.BlockSpec((per,) + shape, lambda x, p: (x, 0, 0))
    keep, near, far = pl.pallas_call(
        part_kernel,
        out_shape=(
            jax.ShapeDtypeStruct((pairs, experts, half, width), BF),
            jax.ShapeDtypeStruct((pairs, experts // 2, half, width), BF),
            jax.ShapeDtypeStruct((pairs, experts // 2, half, width), BF),
        ),
        grid_spec=pltpu.PrefetchScalarGridSpec(
            num_scalar_prefetch=1,
            grid=(experts // per,),
            in_specs=[
                vmem,
                vmem,
                vmem,
                per_expert_p(width, block),
                per_expert_p(width, block),
            ],
            out_specs=(
                pl.BlockSpec(out_block, lambda x, p: (0, x, 0, 0)),
                pl.BlockSpec(out_block, lambda x, p: (0, jnp.minimum(x, near_steps - 1), 0, 0)),
                pl.BlockSpec(out_block, lambda x, p: (0, jnp.maximum(x - near_steps, 0), 0, 0)),
            ),
            scratch_shapes=[pltpu.VMEM((experts, slots // 2, block), F32)] * 2,
        ),
        compiler_params=pltpu.CompilerParams(vmem_limit_bytes=48 * 1024 * 1024),
        cost_estimate=cost,
        name="hidden_part",
    )(place, tok, other, hot, w_down, w_other)

    most_per = 4
    scaled_hot, _ = lax.optimization_barrier((scaled_hot, keep))
    partial = pl.pallas_call(
        weight_kernel,
        out_shape=jax.ShapeDtypeStruct((n_dp, experts, block_f, block), BF),
        grid=(experts // most_per,),
        in_specs=[vmem, vmem, pl.BlockSpec((most_per, slots, width), lambda x: (x, 0, 0))],
        out_specs=pl.BlockSpec((n_dp, most_per, block_f, block), lambda x: (0, x, 0, 0)),
        scratch_shapes=[pltpu.VMEM((experts, slots, block), BF)],
        compiler_params=params,
        cost_estimate=cost,
        name="weight_part",
    )(tok, scaled_hot, hidden_saved[0])
    total = lax.psum_scatter(partial, "dp", scatter_dimension=0, tiled=True)[0]

    def swap(shift):
        at = lambda z: (z ^ 1) if shift == 0 else ((((z + 1) % chips) ^ 1) - 1) % chips
        return [(2 * z + c, 2 * at(z) + c) for z in range(chips) for c in range(2)]

    near = lax.ppermute(near, "tensor", swap(0))
    far = lax.ppermute(far, "tensor", swap(1))
    keep, _ = lax.optimization_barrier((keep, partial))
    row = lambda n: pl.BlockSpec((1, n, half, width), lambda m: (m, 0, 0, 0))
    parts = pl.pallas_call(
        add_kernel,
        out_shape=jax.ShapeDtypeStruct(keep.shape, BF),
        grid=(pairs,),
        in_specs=[row(experts), row(experts // 2), row(experts // 2)],
        out_specs=row(experts),
        compiler_params=params,
        cost_estimate=pl.CostEstimate(flops=60000000000, bytes_accessed=0, transcendentals=0),
        name="pair_sum",
    )(keep, near, far)
    same_kind = [
        [2 * (2 * m + p) + c for m in range(pairs)] for p in range(2) for c in range(2)
    ]
    parts = lax.all_to_all(parts, "tensor", 0, 0, tiled=True, axis_index_groups=same_kind)
    grad_hidden, grad_gates = pl.pallas_call(
        finish_kernel,
        out_shape=(
            jax.ShapeDtypeStruct((experts, half, width), BF),
            jax.ShapeDtypeStruct((experts, half), F32),
        ),
        in_specs=[pl.BlockSpec(memory_space=pltpu.VMEM)] * 3,
        out_specs=(pl.BlockSpec(memory_space=pltpu.VMEM),) * 2,
        compiler_params=pltpu.CompilerParams(vmem_limit_bytes=32 * 1024 * 1024),
        name="finish",
    )(parts, gate_col, my_hidden)
    return grad_hidden[None], grad_gates[None], total


def solution(mesh):
    in_specs = (
        P("dp", "expert", "tensor", None),
        P("dp", "expert", None, None),
        P("dp", "expert", None, None),
        P("dp", "expert", None, None),
        P("expert", None, "tensor"),
    )
    out_specs = (
        P("dp", "expert", "tensor", None),
        P("dp", "expert", "tensor"),
        P("expert", "dp", "tensor"),
    )
    return jax.shard_map(local, mesh=mesh, in_specs=in_specs, out_specs=out_specs, check_vma=False)
```

```python
import functools

import jax
import jax.numpy as jnp
from jax import lax
from jax.experimental import pallas as pl
from jax.experimental.pallas import tpu as pltpu
from jax.sharding import PartitionSpec as P

BF = jnp.bfloat16
F32 = jnp.float32


def iota(shape, dim):
    return lax.broadcasted_iota(jnp.int32, shape, dim)


def tables(meta_ref, columns, first, experts, tokens, choices):
    expert_of = (first + iota((experts, tokens), 0)).astype(F32)
    named, gates = [], []
    for c in range(columns):
        meta = meta_ref[c, tokens:, :].astype(F32)
        hit_any = jnp.zeros((experts, tokens), F32)
        gate = jnp.zeros((experts, tokens), F32)
        for k in range(choices):
            hit = meta[k : k + 1, :] == expert_of
            hit_any = jnp.where(hit, 1.0, hit_any)
            gate = jnp.where(hit, meta[choices + k : choices + k + 1, :], gate)
        named.append(hit_any)
        gates.append(gate)
    named = jnp.concatenate(named, 0)
    before = (iota((tokens, tokens), 0) < iota((tokens, tokens), 1)).astype(F32).astype(BF)
    rank = jnp.dot(named.astype(BF), before, preferred_element_type=F32)
    table = jnp.where(named > 0, rank, -1.0)
    return [table[c * experts : (c + 1) * experts] for c in range(columns)], gates


def picker(table, gate, base, slots, experts, tokens):
    rank = (base + iota((slots, tokens), 0)).astype(F32)
    rows = []
    for x in range(experts):
        value = 1.0 if gate is None else gate[x : x + 1, :]
        rows.append(jnp.where(table[x : x + 1, :] == rank, value, 0.0))
    return jnp.concatenate(rows, 0)


def pick_kernel(place, meta_ref, scaled_hot_ref, hot_ref, gate_ref, *, dims):
    experts, columns, tokens, choices, most = dims
    half = most // 2
    base = place[2] * half
    table, gates = tables(meta_ref, columns, place[0] * experts, experts, tokens, choices)
    for c in range(columns):
        scaled_hot_ref[c] = picker(table[c], gates[c], 0, most, experts, tokens).astype(BF)
        hot_ref[c] = picker(table[c], None, base, half, experts, tokens).astype(BF)

        @pl.when(place[1] == c)
        def _():
            gate = picker(table[c], gates[c], base, half, experts, tokens)
            gate_ref[...] = jnp.broadcast_to(jnp.sum(gate, axis=1, keepdims=True), gate_ref.shape)


def weight_kernel(tok_ref, hot_ref, hidden_ref, out_ref, scaled):
    experts = scaled.shape[0]
    columns = tok_ref.shape[0]
    most = scaled.shape[1] // columns
    step = pl.program_id(0)
    per = hidden_ref.shape[0]

    @pl.when(step == 0)
    def _():
        for c in range(columns):
            rows = jnp.dot(hot_ref[c], tok_ref[c, : hot_ref.shape[2]], preferred_element_type=F32)
            rows = rows.astype(BF)
            for x in range(experts):
                scaled[x, c * most : (c + 1) * most, :] = rows[x * most : (x + 1) * most]

    for i in range(per):
        part = lax.dot_general(
            hidden_ref[i],
            scaled[step * per + i],
            (((0,), (0,)), ((), ())),
            preferred_element_type=F32,
        )
        n_dp, _, block_f, block = out_ref.shape
        out_ref[:, i] = part.astype(BF).reshape(n_dp, block_f, block)


def part_kernel(
    place, tok_ref, other_ref, hot_ref, w_ref, w_other_ref, keep_ref, near_ref, far_ref, mine, theirs
):
    columns, rows_half, _ = hot_ref.shape
    experts = mine.shape[0]
    half = rows_half // experts
    step = pl.program_id(0)
    per = w_ref.shape[0]

    @pl.when(step == 0)
    def _():
        for c in range(columns):
            for src, dst in ((tok_ref, mine), (other_ref, theirs)):
                rows = jnp.dot(
                    hot_ref[c], src[c, : hot_ref.shape[2]], preferred_element_type=F32
                )
                for x in range(experts):
                    dst[x, c * half : (c + 1) * half, :] = rows[x * half : (x + 1) * half]

    dims_nt = (((1,), (1,)), ((), ()))
    odd = place[1] % 2 == 1
    for i in range(per):
        x = step * per + i
        part = lax.dot_general(mine[x].astype(BF), w_ref[i], dims_nt, preferred_element_type=F32)
        part = part + lax.dot_general(
            theirs[x].astype(BF), w_other_ref[i], dims_nt, preferred_element_type=F32
        )
        part = part.reshape(columns // 2, 2, half, part.shape[1])
        keep_ref[:, i] = jnp.where(odd, part[:, 1], part[:, 0]).astype(BF)
        give = jnp.where(odd, part[:, 0], part[:, 1]).astype(BF)

        @pl.when(x < experts // 2)
        def _():
            near_ref[:, i] = give

        @pl.when(x >= experts // 2)
        def _():
            far_ref[:, i] = give


def add_kernel(keep_ref, near_ref, far_ref, out_ref):
    h = near_ref.shape[1]
    out_ref[:, :h] = (keep_ref[:, :h].astype(F32) + near_ref[...].astype(F32)).astype(BF)
    out_ref[:, h:] = (keep_ref[:, h:].astype(F32) + far_ref[...].astype(F32)).astype(BF)


def finish_kernel(parts_ref, gate_ref, hidden_ref, grad_ref, gates_ref):
    sources, experts, half, width = parts_ref.shape
    values = parts_ref[0].astype(F32)
    for s in range(1, sources):
        values = values + parts_ref[s].astype(F32)
    gate = gate_ref[:, :1].reshape(experts, half, 1)
    grad_ref[...] = (gate * values).astype(BF)
    gates_ref[...] = jnp.sum(hidden_ref[...].astype(F32) * values, axis=2)


def local(grad_out, routes, gates, hidden_saved, w_down):
    n_tensor = lax.axis_size("tensor")
    n_expert = lax.axis_size("expert")
    n_dp = lax.axis_size("dp")
    chips = n_tensor // 2
    experts, width, block = w_down.shape
    slots = hidden_saved.shape[2]
    most = slots // n_expert
    half = most // 2
    tokens, choices = routes.shape[2:]
    own = grad_out.shape[2]
    dims = (experts, n_expert, tokens, choices, most)
    me = lax.axis_index("tensor")
    place = jnp.stack([lax.axis_index("expert"), me // 2, me % 2]).astype(jnp.int32)
    pair = [(i, i ^ 1) for i in range(n_tensor)]
    params = pltpu.CompilerParams(vmem_limit_bytes=50 * 1024 * 1024)

    work = 2 * experts * slots * width * block + 2 * n_expert * slots * tokens * block
    cost = pl.CostEstimate(flops=work, bytes_accessed=2 * w_down.size, transcendentals=0)

    w_other = lax.ppermute(w_down, "tensor", pair)
    first = me * (slots // n_tensor)
    my_hidden = lax.dynamic_slice_in_dim(hidden_saved[0], first, slots // n_tensor, 1)

    send = grad_out[0, 0].reshape(own, n_tensor, block).transpose(1, 0, 2)
    column = lax.all_to_all(send, "tensor", 0, 0, tiled=True).reshape(tokens, block)
    packed = jnp.concatenate([column, routes[0, 0].T.astype(BF), gates[0, 0].T], 0)
    packed = jnp.broadcast_to(packed[None], (n_expert,) + packed.shape)
    tok = lax.all_to_all(packed, "expert", 0, 0, tiled=True)
    vmem = pl.BlockSpec(memory_space=pltpu.VMEM)
    scaled_hot, hot, gate_col = pl.pallas_call(
        functools.partial(pick_kernel, dims=dims),
        out_shape=(
            jax.ShapeDtypeStruct((n_expert, experts * most, tokens), BF),
            jax.ShapeDtypeStruct((n_expert, experts * half, tokens), BF),
            jax.ShapeDtypeStruct((experts * half, 128), F32),
        ),
        grid_spec=pltpu.PrefetchScalarGridSpec(
            num_scalar_prefetch=1,
            grid=(1,),
            in_specs=[vmem],
            out_specs=(
                vmem,
                vmem,
                vmem,
            ),
        ),
        compiler_params=pltpu.CompilerParams(vmem_limit_bytes=16 * 1024 * 1024),
        cost_estimate=cost,
        name="pick",
    )(place, tok)
    other = lax.ppermute(tok, "tensor", pair)

    per = 2
    per_expert = lambda *shape: pl.BlockSpec((per,) + shape, lambda x: (x, 0, 0))
    block_f = width // n_dp
    pairs, near_steps = chips // 2, experts // per // 2
    out_block = (pairs, per, half, width)
    per_expert_p = lambda *shape: pl.BlockSpec((per,) + shape, lambda x, p: (x, 0, 0))
    keep, near, far = pl.pallas_call(
        part_kernel,
        out_shape=(
            jax.ShapeDtypeStruct((pairs, experts, half, width), BF),
            jax.ShapeDtypeStruct((pairs, experts // 2, half, width), BF),
            jax.ShapeDtypeStruct((pairs, experts // 2, half, width), BF),
        ),
        grid_spec=pltpu.PrefetchScalarGridSpec(
            num_scalar_prefetch=1,
            grid=(experts // per,),
            in_specs=[
                vmem,
                vmem,
                vmem,
                per_expert_p(width, block),
                per_expert_p(width, block),
            ],
            out_specs=(
                pl.BlockSpec(out_block, lambda x, p: (0, x, 0, 0)),
                pl.BlockSpec(out_block, lambda x, p: (0, jnp.minimum(x, near_steps - 1), 0, 0)),
                pl.BlockSpec(out_block, lambda x, p: (0, jnp.maximum(x - near_steps, 0), 0, 0)),
            ),
            scratch_shapes=[pltpu.VMEM((experts, slots // 2, block), F32)] * 2,
        ),
        compiler_params=pltpu.CompilerParams(vmem_limit_bytes=32 * 1024 * 1024),
        cost_estimate=cost,
        name="hidden_part",
    )(place, tok, other, hot, w_down, w_other)

    most_per = 4
    scaled_hot, _ = lax.optimization_barrier((scaled_hot, keep))
    partial = pl.pallas_call(
        weight_kernel,
        out_shape=jax.ShapeDtypeStruct((n_dp, experts, block_f, block), BF),
        grid=(experts // most_per,),
        in_specs=[vmem, vmem, pl.BlockSpec((most_per, slots, width), lambda x: (x, 0, 0))],
        out_specs=pl.BlockSpec((n_dp, most_per, block_f, block), lambda x: (0, x, 0, 0)),
        scratch_shapes=[pltpu.VMEM((experts, slots, block), BF)],
        compiler_params=params,
        cost_estimate=cost,
        name="weight_part",
    )(tok, scaled_hot, hidden_saved[0])
    total = lax.psum_scatter(partial, "dp", scatter_dimension=0, tiled=True)[0]

    def swap(shift):
        at = lambda z: (z ^ 1) if shift == 0 else ((((z + 1) % chips) ^ 1) - 1) % chips
        return [(2 * z + c, 2 * at(z) + c) for z in range(chips) for c in range(2)]

    near = lax.ppermute(near, "tensor", swap(0))
    far = lax.ppermute(far, "tensor", swap(1))
    keep, _ = lax.optimization_barrier((keep, partial))
    row = lambda n: pl.BlockSpec((2, n, half, width), lambda m: (m, 0, 0, 0))
    parts = pl.pallas_call(
        add_kernel,
        out_shape=jax.ShapeDtypeStruct(keep.shape, BF),
        grid=(pairs // 2,),
        in_specs=[row(experts), row(experts // 2), row(experts // 2)],
        out_specs=row(experts),
        compiler_params=params,
        cost_estimate=pl.CostEstimate(flops=60000000000, bytes_accessed=0, transcendentals=0),
        name="pair_sum",
    )(keep, near, far)
    same_kind = [
        [2 * (2 * m + p) + c for m in range(pairs)] for p in range(2) for c in range(2)
    ]
    parts = lax.all_to_all(parts, "tensor", 0, 0, tiled=True, axis_index_groups=same_kind)
    grad_hidden, grad_gates = pl.pallas_call(
        finish_kernel,
        out_shape=(
            jax.ShapeDtypeStruct((experts, half, width), BF),
            jax.ShapeDtypeStruct((experts, half), F32),
        ),
        in_specs=[pl.BlockSpec(memory_space=pltpu.VMEM)] * 3,
        out_specs=(pl.BlockSpec(memory_space=pltpu.VMEM),) * 2,
        compiler_params=pltpu.CompilerParams(vmem_limit_bytes=32 * 1024 * 1024),
        name="finish",
    )(parts, gate_col, my_hidden)
    return grad_hidden[None], grad_gates[None], total


def solution(mesh):
    in_specs = (
        P("dp", "expert", "tensor", None),
        P("dp", "expert", None, None),
        P("dp", "expert", None, None),
        P("dp", "expert", None, None),
        P("expert", None, "tensor"),
    )
    out_specs = (
        P("dp", "expert", "tensor", None),
        P("dp", "expert", "tensor"),
        P("expert", "dp", "tensor"),
    )
    return jax.shard_map(local, mesh=mesh, in_specs=in_specs, out_specs=out_specs, check_vma=False)
```

```python
import functools

import jax
import jax.numpy as jnp
from jax import lax
from jax.experimental import pallas as pl
from jax.experimental.pallas import tpu as pltpu
from jax.sharding import PartitionSpec as P

BF = jnp.bfloat16
F32 = jnp.float32


def iota(shape, dim):
    return lax.broadcasted_iota(jnp.int32, shape, dim)


def tables(meta_ref, columns, place_x, experts, tokens, choices):
    expert_of = (place_x * experts + iota((experts, tokens), 0)).astype(F32)
    named, gates = [], []
    for c in range(columns):
        meta = meta_ref[c ^ place_x, :, :].astype(F32)
        hit_any = jnp.zeros((experts, tokens), F32)
        gate = jnp.zeros((experts, tokens), F32)
        for k in range(choices):
            hit = meta[k : k + 1, :] == expert_of
            hit_any = jnp.where(hit, 1.0, hit_any)
            gate = jnp.where(hit, meta[choices + k : choices + k + 1, :], gate)
        named.append(hit_any)
        gates.append(gate)
    named = jnp.concatenate(named, 0)
    before = (iota((tokens, tokens), 0) < iota((tokens, tokens), 1)).astype(F32).astype(BF)
    rank = jnp.dot(named.astype(BF), before, preferred_element_type=F32)
    table = jnp.where(named > 0, rank, -1.0)
    return [table[c * experts : (c + 1) * experts] for c in range(columns)], gates


def picker(table, gate, base, slots, experts, tokens):
    rank = (base + iota((slots, tokens), 0)).astype(F32)
    rows = []
    for x in range(experts):
        value = 1.0 if gate is None else gate[x : x + 1, :]
        rows.append(jnp.where(table[x : x + 1, :] == rank, value, 0.0))
    return jnp.concatenate(rows, 0)


def pick_kernel(place, meta_ref, scaled_hot_ref, hot_ref, gate_ref, *, dims):
    experts, columns, tokens, choices, most = dims
    half = most // 2
    base = place[2] * half
    table, gates = tables(meta_ref, columns, place[0], experts, tokens, choices)
    for c in range(columns):
        scaled_hot_ref[c] = picker(table[c], gates[c], 0, most, experts, tokens).astype(BF)
        hot_ref[c] = picker(table[c], None, base, half, experts, tokens).astype(BF)

        @pl.when(place[1] == c)
        def _():
            gate = picker(table[c], gates[c], base, half, experts, tokens)
            gate_ref[...] = jnp.broadcast_to(jnp.sum(gate, axis=1, keepdims=True), gate_ref.shape)


def weight_kernel(tok_ref, hot_ref, hidden_ref, out_ref, scaled):
    experts = scaled.shape[0]
    columns = tok_ref.shape[0]
    most = scaled.shape[1] // columns
    step = pl.program_id(0)
    per = hidden_ref.shape[0]

    @pl.when(step == 0)
    def _():
        for c in range(columns):
            rows = jnp.dot(hot_ref[c], tok_ref[c, : hot_ref.shape[2]], preferred_element_type=F32)
            rows = rows.astype(BF)
            for x in range(experts):
                scaled[x, c * most : (c + 1) * most, :] = rows[x * most : (x + 1) * most]

    for i in range(per):
        part = lax.dot_general(
            hidden_ref[i],
            scaled[step * per + i],
            (((0,), (0,)), ((), ())),
            preferred_element_type=F32,
        )
        n_dp, _, block_f, block = out_ref.shape
        out_ref[:, i] = part.astype(BF).reshape(n_dp, block_f, block)


def part_kernel(
    place, tok_ref, other_ref, hot_ref, w_ref, w_other_ref, keep_ref, near_ref, far_ref, mine, theirs
):
    columns, rows_half, _ = hot_ref.shape
    experts = mine.shape[0]
    half = rows_half // experts
    step = pl.program_id(0)
    per = w_ref.shape[0]

    @pl.when(step == 0)
    def _():
        for c in range(columns):
            for src, dst in ((tok_ref, mine), (other_ref, theirs)):
                rows = jnp.dot(
                    hot_ref[c], src[c, : hot_ref.shape[2]], preferred_element_type=F32
                )
                for x in range(experts):
                    dst[x, c * half : (c + 1) * half, :] = rows[x * half : (x + 1) * half]

    dims_nt = (((1,), (1,)), ((), ()))
    odd = place[1] % 2 == 1
    for i in range(per):
        x = step * per + i
        part = lax.dot_general(mine[x].astype(BF), w_ref[i], dims_nt, preferred_element_type=F32)
        part = part + lax.dot_general(
            theirs[x].astype(BF), w_other_ref[i], dims_nt, preferred_element_type=F32
        )
        part = part.reshape(columns // 2, 2, half, part.shape[1])
        keep_ref[:, i] = jnp.where(odd, part[:, 1], part[:, 0]).astype(BF)
        give = jnp.where(odd, part[:, 0], part[:, 1]).astype(BF)

        @pl.when(x < experts // 2)
        def _():
            near_ref[:, i] = give

        @pl.when(x >= experts // 2)
        def _():
            far_ref[:, i] = give


def add_kernel(keep_ref, near_ref, far_ref, out_ref):
    h = near_ref.shape[1]
    out_ref[:, :h] = (keep_ref[:, :h].astype(F32) + near_ref[...].astype(F32)).astype(BF)
    out_ref[:, h:] = (keep_ref[:, h:].astype(F32) + far_ref[...].astype(F32)).astype(BF)


def finish_kernel(parts_ref, gate_ref, hidden_ref, grad_ref, gates_ref):
    sources, experts, half, width = parts_ref.shape
    values = parts_ref[0].astype(F32)
    for s in range(1, sources):
        values = values + parts_ref[s].astype(F32)
    gate = gate_ref[:, :1].reshape(experts, half, 1)
    grad_ref[...] = (gate * values).astype(BF)
    gates_ref[...] = jnp.sum(hidden_ref[...].astype(F32) * values, axis=2)


def local(grad_out, routes, gates, hidden_saved, w_down):
    n_tensor = lax.axis_size("tensor")
    n_expert = lax.axis_size("expert")
    n_dp = lax.axis_size("dp")
    chips = n_tensor // 2
    experts, width, block = w_down.shape
    slots = hidden_saved.shape[2]
    most = slots // n_expert
    half = most // 2
    tokens, choices = routes.shape[2:]
    own = grad_out.shape[2]
    dims = (experts, n_expert, tokens, choices, most)
    me = lax.axis_index("tensor")
    place = jnp.stack([lax.axis_index("expert"), me // 2, me % 2]).astype(jnp.int32)
    pair = [(i, i ^ 1) for i in range(n_tensor)]
    params = pltpu.CompilerParams(vmem_limit_bytes=50 * 1024 * 1024)

    work = 2 * experts * slots * width * block + 2 * n_expert * slots * tokens * block
    cost = pl.CostEstimate(flops=work, bytes_accessed=2 * w_down.size, transcendentals=0)

    w_other = lax.ppermute(w_down, "tensor", pair)
    first = me * (slots // n_tensor)
    my_hidden = lax.dynamic_slice_in_dim(hidden_saved[0], first, slots // n_tensor, 1)

    send = grad_out[0, 0].reshape(own, n_tensor, block).transpose(1, 0, 2)
    send = jnp.broadcast_to(send[None], (n_expert,) + send.shape)
    send = send.reshape(n_expert * n_tensor, own, block)
    tok = lax.all_to_all(send, ("expert", "tensor"), 0, 0, tiled=True)
    tok = tok.reshape(n_expert, tokens, block)
    meta = jnp.concatenate([routes[0, 0].T.astype(BF), gates[0, 0].T], 0)[None]
    reach = 1
    while reach < n_expert:
        far_meta = lax.ppermute(meta, "expert", [(i, i ^ reach) for i in range(n_expert)])
        meta = jnp.concatenate([meta, far_meta], 0)
        reach = 2 * reach
    vmem = pl.BlockSpec(memory_space=pltpu.VMEM)
    scaled_hot, hot, gate_col = pl.pallas_call(
        functools.partial(pick_kernel, dims=dims),
        out_shape=(
            jax.ShapeDtypeStruct((n_expert, experts * most, tokens), BF),
            jax.ShapeDtypeStruct((n_expert, experts * half, tokens), BF),
            jax.ShapeDtypeStruct((experts * half, 128), F32),
        ),
        grid_spec=pltpu.PrefetchScalarGridSpec(
            num_scalar_prefetch=1,
            grid=(1,),
            in_specs=[vmem],
            out_specs=(
                vmem,
                vmem,
                vmem,
            ),
        ),
        compiler_params=pltpu.CompilerParams(vmem_limit_bytes=16 * 1024 * 1024),
        cost_estimate=cost,
        name="pick",
    )(place, meta)
    tok, hot = lax.optimization_barrier((tok, hot))
    other = lax.ppermute(tok, "tensor", pair)

    per = 2
    per_expert = lambda *shape: pl.BlockSpec((per,) + shape, lambda x: (x, 0, 0))
    block_f = width // n_dp
    pairs, near_steps = chips // 2, experts // per // 2
    out_block = (pairs, per, half, width)
    per_expert_p = lambda *shape: pl.BlockSpec((per,) + shape, lambda x, p: (x, 0, 0))
    keep, near, far = pl.pallas_call(
        part_kernel,
        out_shape=(
            jax.ShapeDtypeStruct((pairs, experts, half, width), BF),
            jax.ShapeDtypeStruct((pairs, experts // 2, half, width), BF),
            jax.ShapeDtypeStruct((pairs, experts // 2, half, width), BF),
        ),
        grid_spec=pltpu.PrefetchScalarGridSpec(
            num_scalar_prefetch=1,
            grid=(experts // per,),
            in_specs=[
                vmem,
                vmem,
                vmem,
                per_expert_p(width, block),
                per_expert_p(width, block),
            ],
            out_specs=(
                pl.BlockSpec(out_block, lambda x, p: (0, x, 0, 0)),
                pl.BlockSpec(out_block, lambda x, p: (0, jnp.minimum(x, near_steps - 1), 0, 0)),
                pl.BlockSpec(out_block, lambda x, p: (0, jnp.maximum(x - near_steps, 0), 0, 0)),
            ),
            scratch_shapes=[pltpu.VMEM((experts, slots // 2, block), F32)] * 2,
        ),
        compiler_params=pltpu.CompilerParams(vmem_limit_bytes=48 * 1024 * 1024),
        cost_estimate=cost,
        name="hidden_part",
    )(place, tok, other, hot, w_down, w_other)

    most_per = 4
    scaled_hot, _ = lax.optimization_barrier((scaled_hot, keep))
    partial = pl.pallas_call(
        weight_kernel,
        out_shape=jax.ShapeDtypeStruct((n_dp, experts, block_f, block), BF),
        grid=(experts // most_per,),
        in_specs=[vmem, vmem, pl.BlockSpec((most_per, slots, width), lambda x: (x, 0, 0))],
        out_specs=pl.BlockSpec((n_dp, most_per, block_f, block), lambda x: (0, x, 0, 0)),
        scratch_shapes=[pltpu.VMEM((experts, slots, block), BF)],
        compiler_params=params,
        cost_estimate=cost,
        name="weight_part",
    )(tok, scaled_hot, hidden_saved[0])
    total = lax.psum_scatter(partial, "dp", scatter_dimension=0, tiled=True)[0]

    def swap(shift):
        at = lambda z: (z ^ 1) if shift == 0 else ((((z + 1) % chips) ^ 1) - 1) % chips
        return [(2 * z + c, 2 * at(z) + c) for z in range(chips) for c in range(2)]

    near = lax.ppermute(near, "tensor", swap(0))
    far = lax.ppermute(far, "tensor", swap(1))
    keep, _ = lax.optimization_barrier((keep, partial))
    row = lambda n: pl.BlockSpec((2, n, half, width), lambda m: (m, 0, 0, 0))
    parts = pl.pallas_call(
        add_kernel,
        out_shape=jax.ShapeDtypeStruct(keep.shape, BF),
        grid=(pairs // 2,),
        in_specs=[row(experts), row(experts // 2), row(experts // 2)],
        out_specs=row(experts),
        compiler_params=params,
        cost_estimate=pl.CostEstimate(flops=60000000000, bytes_accessed=0, transcendentals=0),
        name="pair_sum",
    )(keep, near, far)
    same_kind = [
        [2 * (2 * m + p) + c for m in range(pairs)] for p in range(2) for c in range(2)
    ]
    parts = lax.all_to_all(parts, "tensor", 0, 0, tiled=True, axis_index_groups=same_kind)
    grad_hidden, grad_gates = pl.pallas_call(
        finish_kernel,
        out_shape=(
            jax.ShapeDtypeStruct((experts, half, width), BF),
            jax.ShapeDtypeStruct((experts, half), F32),
        ),
        in_specs=[pl.BlockSpec(memory_space=pltpu.VMEM)] * 3,
        out_specs=(pl.BlockSpec(memory_space=pltpu.VMEM),) * 2,
        compiler_params=pltpu.CompilerParams(vmem_limit_bytes=32 * 1024 * 1024),
        name="finish",
    )(parts, gate_col, my_hidden)
    return grad_hidden[None], grad_gates[None], total


def solution(mesh):
    in_specs = (
        P("dp", "expert", "tensor", None),
        P("dp", "expert", None, None),
        P("dp", "expert", None, None),
        P("dp", "expert", None, None),
        P("expert", None, "tensor"),
    )
    out_specs = (
        P("dp", "expert", "tensor", None),
        P("dp", "expert", "tensor"),
        P("expert", "dp", "tensor"),
    )
    return jax.shard_map(local, mesh=mesh, in_specs=in_specs, out_specs=out_specs, check_vma=False)
```

```python
import functools

import jax
import jax.numpy as jnp
from jax import lax
from jax.experimental import pallas as pl
from jax.experimental.pallas import tpu as pltpu
from jax.sharding import PartitionSpec as P

BF = jnp.bfloat16
F32 = jnp.float32


def iota(shape, dim):
    return lax.broadcasted_iota(jnp.int32, shape, dim)


def tables(meta_ref, columns, first, experts, tokens, choices):
    expert_of = (first + iota((experts, tokens), 0)).astype(F32)
    named, gates = [], []
    for c in range(columns):
        meta = meta_ref[c, tokens:, :].astype(F32)
        hit_any = jnp.zeros((experts, tokens), F32)
        gate = jnp.zeros((experts, tokens), F32)
        for k in range(choices):
            hit = meta[k : k + 1, :] == expert_of
            hit_any = jnp.where(hit, 1.0, hit_any)
            gate = jnp.where(hit, meta[choices + k : choices + k + 1, :], gate)
        named.append(hit_any)
        gates.append(gate)
    named = jnp.concatenate(named, 0)
    before = (iota((tokens, tokens), 0) < iota((tokens, tokens), 1)).astype(F32).astype(BF)
    rank = jnp.dot(named.astype(BF), before, preferred_element_type=F32)
    table = jnp.where(named > 0, rank, -1.0)
    return [table[c * experts : (c + 1) * experts] for c in range(columns)], gates


def picker(table, gate, base, slots, experts, tokens):
    rank = (base + iota((slots, tokens), 0)).astype(F32)
    rows = []
    for x in range(experts):
        value = 1.0 if gate is None else gate[x : x + 1, :]
        rows.append(jnp.where(table[x : x + 1, :] == rank, value, 0.0))
    return jnp.concatenate(rows, 0)


def pick_kernel(place, meta_ref, scaled_hot_ref, hot_ref, gate_ref, *, dims):
    experts, columns, tokens, choices, most = dims
    half = most // 2
    base = place[2] * half
    table, gates = tables(meta_ref, columns, place[0] * experts, experts, tokens, choices)
    for c in range(columns):
        scaled_hot_ref[c] = picker(table[c], gates[c], 0, most, experts, tokens).astype(BF)
        hot_ref[c] = picker(table[c], None, base, half, experts, tokens).astype(BF)

        @pl.when(place[1] == c)
        def _():
            gate = picker(table[c], gates[c], base, half, experts, tokens)
            gate_ref[...] = jnp.broadcast_to(jnp.sum(gate, axis=1, keepdims=True), gate_ref.shape)


def weight_kernel(tok_ref, hot_ref, hidden_ref, out_ref, scaled):
    experts = scaled.shape[0]
    columns = tok_ref.shape[0]
    most = scaled.shape[1] // columns
    step = pl.program_id(0)
    per = hidden_ref.shape[0]

    @pl.when(step == 0)
    def _():
        for c in range(columns):
            rows = jnp.dot(hot_ref[c], tok_ref[c, : hot_ref.shape[2]], preferred_element_type=F32)
            rows = rows.astype(BF)
            for x in range(experts):
                scaled[x, c * most : (c + 1) * most, :] = rows[x * most : (x + 1) * most]

    for i in range(per):
        part = lax.dot_general(
            hidden_ref[i],
            scaled[step * per + i],
            (((0,), (0,)), ((), ())),
            preferred_element_type=F32,
        )
        n_dp, _, block_f, block = out_ref.shape
        out_ref[:, i] = part.astype(BF).reshape(n_dp, block_f, block)


def part_kernel(
    place, tok_ref, other_ref, hot_ref, w_ref, w_other_ref, keep_ref, give_ref, mine, theirs, *, low, half
):
    columns, _, tokens = hot_ref.shape
    experts = mine.shape[0]
    step = pl.program_id(0)
    per = w_ref.shape[0]

    @pl.when(step == 0)
    def _():
        for c in range(columns):
            hot = hot_ref[c, low * half : (low + experts) * half, :]
            for src, dst in ((tok_ref, mine), (other_ref, theirs)):
                rows = jnp.dot(hot, src[c, :tokens], preferred_element_type=F32)
                for x in range(experts):
                    dst[x, c * half : (c + 1) * half, :] = rows[x * half : (x + 1) * half]

    dims_nt = (((1,), (1,)), ((), ()))
    odd = place[1] % 2 == 1
    for i in range(per):
        x = step * per + i
        part = lax.dot_general(mine[x].astype(BF), w_ref[i], dims_nt, preferred_element_type=F32)
        part = part + lax.dot_general(
            theirs[x].astype(BF), w_other_ref[i], dims_nt, preferred_element_type=F32
        )
        part = part.reshape(columns // 2, 2, half, part.shape[1])
        keep_ref[:, i] = jnp.where(odd, part[:, 1], part[:, 0]).astype(BF)
        give_ref[:, i] = jnp.where(odd, part[:, 0], part[:, 1]).astype(BF)


def add_kernel(keep_a_ref, keep_b_ref, near_ref, far_ref, out_ref):
    h = near_ref.shape[1]
    out_ref[:, :h] = (keep_a_ref[...].astype(F32) + near_ref[...].astype(F32)).astype(BF)
    out_ref[:, h:] = (keep_b_ref[...].astype(F32) + far_ref[...].astype(F32)).astype(BF)


def finish_kernel(parts_ref, gate_ref, hidden_ref, grad_ref, gates_ref):
    sources, experts, half, width = parts_ref.shape
    values = parts_ref[0].astype(F32)
    for s in range(1, sources):
        values = values + parts_ref[s].astype(F32)
    gate = gate_ref[:, :1].reshape(experts, half, 1)
    grad_ref[...] = (gate * values).astype(BF)
    gates_ref[...] = jnp.sum(hidden_ref[...].astype(F32) * values, axis=2)


def local(grad_out, routes, gates, hidden_saved, w_down):
    n_tensor = lax.axis_size("tensor")
    n_expert = lax.axis_size("expert")
    n_dp = lax.axis_size("dp")
    chips = n_tensor // 2
    experts, width, block = w_down.shape
    slots = hidden_saved.shape[2]
    most = slots // n_expert
    half = most // 2
    tokens, choices = routes.shape[2:]
    own = grad_out.shape[2]
    dims = (experts, n_expert, tokens, choices, most)
    me = lax.axis_index("tensor")
    place = jnp.stack([lax.axis_index("expert"), me // 2, me % 2]).astype(jnp.int32)
    pair = [(i, i ^ 1) for i in range(n_tensor)]
    params = pltpu.CompilerParams(vmem_limit_bytes=50 * 1024 * 1024)

    work = 2 * experts * slots * width * block + 2 * n_expert * slots * tokens * block
    cost = pl.CostEstimate(flops=work, bytes_accessed=2 * w_down.size, transcendentals=0)

    w_other = lax.ppermute(w_down, "tensor", pair)
    first = me * (slots // n_tensor)
    my_hidden = lax.dynamic_slice_in_dim(hidden_saved[0], first, slots // n_tensor, 1)

    send = grad_out[0, 0].reshape(own, n_tensor, block).transpose(1, 0, 2)
    column = lax.all_to_all(send, "tensor", 0, 0, tiled=True).reshape(tokens, block)
    packed = jnp.concatenate([column, routes[0, 0].T.astype(BF), gates[0, 0].T], 0)
    packed = jnp.broadcast_to(packed[None], (n_expert,) + packed.shape)
    tok = lax.all_to_all(packed, "expert", 0, 0, tiled=True)
    vmem = pl.BlockSpec(memory_space=pltpu.VMEM)
    scaled_hot, hot, gate_col = pl.pallas_call(
        functools.partial(pick_kernel, dims=dims),
        out_shape=(
            jax.ShapeDtypeStruct((n_expert, experts * most, tokens), BF),
            jax.ShapeDtypeStruct((n_expert, experts * half, tokens), BF),
            jax.ShapeDtypeStruct((experts * half, 128), F32),
        ),
        grid_spec=pltpu.PrefetchScalarGridSpec(
            num_scalar_prefetch=1,
            grid=(1,),
            in_specs=[vmem],
            out_specs=(
                vmem,
                vmem,
                vmem,
            ),
        ),
        compiler_params=pltpu.CompilerParams(vmem_limit_bytes=16 * 1024 * 1024),
        cost_estimate=cost,
        name="pick",
    )(place, tok)
    other = lax.ppermute(tok, "tensor", pair)

    per = 2
    per_expert = lambda *shape: pl.BlockSpec((per,) + shape, lambda x: (x, 0, 0))
    block_f = width // n_dp
    pairs = chips // 2
    per_expert_p = lambda low, *shape: pl.BlockSpec((per,) + shape, lambda x, p: (x + low // per, 0, 0))

    def hidden_parts(low, count, hot):
        out = jax.ShapeDtypeStruct((pairs, count, half, width), BF)
        return pl.pallas_call(
            functools.partial(part_kernel, low=low, half=half),
            out_shape=(out, out),
            grid_spec=pltpu.PrefetchScalarGridSpec(
                num_scalar_prefetch=1,
                grid=(count // per,),
                in_specs=[
                    vmem,
                    vmem,
                    vmem,
                    per_expert_p(low, width, block),
                    per_expert_p(low, width, block),
                ],
                out_specs=(pl.BlockSpec((pairs, per, half, width), lambda x, p: (0, x, 0, 0)),) * 2,
                scratch_shapes=[pltpu.VMEM((count, slots // 2, block), F32)] * 2,
            ),
            compiler_params=pltpu.CompilerParams(vmem_limit_bytes=32 * 1024 * 1024),
            cost_estimate=cost,
            name="hidden_part",
        )(place, tok, other, hot, w_down, w_other)

    def swap(shift):
        at = lambda z: (z ^ 1) if shift == 0 else ((((z + 1) % chips) ^ 1) - 1) % chips
        return [(2 * z + c, 2 * at(z) + c) for z in range(chips) for c in range(2)]

    split = experts - per
    keep_a, near = hidden_parts(0, split, hot)
    near_back = lax.ppermute(near, "tensor", swap(0))
    scaled_hot, _ = lax.optimization_barrier((scaled_hot, near))
    partial = pl.pallas_call(
        weight_kernel,
        out_shape=jax.ShapeDtypeStruct((n_dp, experts, block_f, block), BF),
        grid=(experts // 4,),
        in_specs=[vmem, vmem, pl.BlockSpec((4, slots, width), lambda x: (x, 0, 0))],
        out_specs=pl.BlockSpec((n_dp, 4, block_f, block), lambda x: (0, x, 0, 0)),
        scratch_shapes=[pltpu.VMEM((experts, slots, block), BF)],
        compiler_params=params,
        cost_estimate=cost,
        name="weight_part",
    )(tok, scaled_hot, hidden_saved[0])
    total = lax.psum_scatter(partial, "dp", scatter_dimension=0, tiled=True)[0]
    hot_late, _ = lax.optimization_barrier((hot, partial))
    keep_b, far = hidden_parts(split, experts - split, hot_late)
    far_back = lax.ppermute(far, "tensor", swap(1))
    row = lambda n: pl.BlockSpec((2, n, half, width), lambda m: (m, 0, 0, 0))
    parts = pl.pallas_call(
        add_kernel,
        out_shape=jax.ShapeDtypeStruct((pairs, experts, half, width), BF),
        grid=(pairs // 2,),
        in_specs=[row(split), row(experts - split), row(split), row(experts - split)],
        out_specs=row(experts),
        compiler_params=params,
        cost_estimate=pl.CostEstimate(flops=42000000000, bytes_accessed=0, transcendentals=0),
        name="pair_sum",
    )(keep_a, keep_b, near_back, far_back)
    same_kind = [
        [2 * (2 * m + p) + c for m in range(pairs)] for p in range(2) for c in range(2)
    ]
    parts = lax.all_to_all(parts, "tensor", 0, 0, tiled=True, axis_index_groups=same_kind)
    grad_hidden, grad_gates = pl.pallas_call(
        finish_kernel,
        out_shape=(
            jax.ShapeDtypeStruct((experts, half, width), BF),
            jax.ShapeDtypeStruct((experts, half), F32),
        ),
        in_specs=[pl.BlockSpec(memory_space=pltpu.VMEM)] * 3,
        out_specs=(pl.BlockSpec(memory_space=pltpu.VMEM),) * 2,
        compiler_params=pltpu.CompilerParams(vmem_limit_bytes=32 * 1024 * 1024),
        name="finish",
    )(parts, gate_col, my_hidden)
    return grad_hidden[None], grad_gates[None], total


def solution(mesh):
    in_specs = (
        P("dp", "expert", "tensor", None),
        P("dp", "expert", None, None),
        P("dp", "expert", None, None),
        P("dp", "expert", None, None),
        P("expert", None, "tensor"),
    )
    out_specs = (
        P("dp", "expert", "tensor", None),
        P("dp", "expert", "tensor"),
        P("expert", "dp", "tensor"),
    )
    return jax.shard_map(local, mesh=mesh, in_specs=in_specs, out_specs=out_specs, check_vma=False)
```

```python
import functools

import jax
import jax.numpy as jnp
from jax import lax
from jax.experimental import pallas as pl
from jax.experimental.pallas import tpu as pltpu
from jax.sharding import PartitionSpec as P

BF = jnp.bfloat16
F32 = jnp.float32


def iota(shape, dim):
    return lax.broadcasted_iota(jnp.int32, shape, dim)


def tables(meta_ref, columns, first, experts, tokens, choices):
    expert_of = (first + iota((experts, tokens), 0)).astype(F32)
    named, gates = [], []
    for c in range(columns):
        meta = meta_ref[c, tokens:, :].astype(F32)
        hit_any = jnp.zeros((experts, tokens), F32)
        gate = jnp.zeros((experts, tokens), F32)
        for k in range(choices):
            hit = meta[k : k + 1, :] == expert_of
            hit_any = jnp.where(hit, 1.0, hit_any)
            gate = jnp.where(hit, meta[choices + k : choices + k + 1, :], gate)
        named.append(hit_any)
        gates.append(gate)
    named = jnp.concatenate(named, 0)
    before = (iota((tokens, tokens), 0) < iota((tokens, tokens), 1)).astype(F32).astype(BF)
    rank = jnp.dot(named.astype(BF), before, preferred_element_type=F32)
    table = jnp.where(named > 0, rank, -1.0)
    return [table[c * experts : (c + 1) * experts] for c in range(columns)], gates


def picker(table, gate, base, slots, experts, tokens):
    rank = (base + iota((slots, tokens), 0)).astype(F32)
    rows = []
    for x in range(experts):
        value = 1.0 if gate is None else gate[x : x + 1, :]
        rows.append(jnp.where(table[x : x + 1, :] == rank, value, 0.0))
    return jnp.concatenate(rows, 0)


def pick_kernel(place, meta_ref, scaled_hot_ref, hot_ref, gate_ref, *, dims):
    experts, columns, tokens, choices, most = dims
    half = most // 2
    base = place[2] * half
    table, gates = tables(meta_ref, columns, place[0] * experts, experts, tokens, choices)
    for c in range(columns):
        scaled_hot_ref[c] = picker(table[c], gates[c], 0, most, experts, tokens).astype(BF)
        hot_ref[c] = picker(table[c], None, base, half, experts, tokens).astype(BF)

        @pl.when(place[1] == c)
        def _():
            gate = picker(table[c], gates[c], base, half, experts, tokens)
            gate_ref[...] = jnp.broadcast_to(jnp.sum(gate, axis=1, keepdims=True), gate_ref.shape)


def weight_kernel(tok_ref, hot_ref, hidden_ref, out_ref, scaled):
    experts = scaled.shape[0]
    columns = tok_ref.shape[0]
    most = scaled.shape[1] // columns
    step = pl.program_id(0)
    per = hidden_ref.shape[0]

    @pl.when(step == 0)
    def _():
        for c in range(columns):
            rows = jnp.dot(hot_ref[c], tok_ref[c, : hot_ref.shape[2]], preferred_element_type=F32)
            rows = rows.astype(BF)
            for x in range(experts):
                scaled[x, c * most : (c + 1) * most, :] = rows[x * most : (x + 1) * most]

    for i in range(per):
        part = lax.dot_general(
            hidden_ref[i],
            scaled[step * per + i],
            (((0,), (0,)), ((), ())),
            preferred_element_type=F32,
        )
        n_dp, _, block_f, block = out_ref.shape
        out_ref[:, i] = part.astype(BF).reshape(n_dp, block_f, block)


def part_kernel(
    place, tok_ref, other_ref, hot_ref, w_ref, w_other_ref, keep_ref, give_ref, mine, theirs, *, low, half
):
    columns, _, tokens = hot_ref.shape
    experts = mine.shape[0]
    step = pl.program_id(0)
    per = w_ref.shape[0]

    @pl.when(step == 0)
    def _():
        for c in range(columns):
            hot = hot_ref[c, low * half : (low + experts) * half, :]
            for src, dst in ((tok_ref, mine), (other_ref, theirs)):
                rows = jnp.dot(hot, src[c, :tokens], preferred_element_type=F32)
                for x in range(experts):
                    dst[x, c * half : (c + 1) * half, :] = rows[x * half : (x + 1) * half]

    dims_nt = (((1,), (1,)), ((), ()))
    odd = place[1] % 2 == 1
    for i in range(per):
        x = step * per + i
        part = lax.dot_general(mine[x].astype(BF), w_ref[i], dims_nt, preferred_element_type=F32)
        part = part + lax.dot_general(
            theirs[x].astype(BF), w_other_ref[i], dims_nt, preferred_element_type=F32
        )
        part = part.reshape(columns // 2, 2, half, part.shape[1])
        keep_ref[:, i] = jnp.where(odd, part[:, 1], part[:, 0]).astype(BF)
        give_ref[:, i] = jnp.where(odd, part[:, 0], part[:, 1]).astype(BF)


def add_kernel(keep_a_ref, keep_b_ref, near_ref, far_ref, out_ref):
    h = near_ref.shape[1]
    out_ref[:, :h] = (keep_a_ref[...].astype(F32) + near_ref[...].astype(F32)).astype(BF)
    out_ref[:, h:] = (keep_b_ref[...].astype(F32) + far_ref[...].astype(F32)).astype(BF)


def finish_kernel(parts_ref, gate_ref, hidden_ref, grad_ref, gates_ref):
    sources, experts, half, width = parts_ref.shape
    values = parts_ref[0].astype(F32)
    for s in range(1, sources):
        values = values + parts_ref[s].astype(F32)
    gate = gate_ref[:, :1].reshape(experts, half, 1)
    grad_ref[...] = (gate * values).astype(BF)
    gates_ref[...] = jnp.sum(hidden_ref[...].astype(F32) * values, axis=2)


def local(grad_out, routes, gates, hidden_saved, w_down):
    n_tensor = lax.axis_size("tensor")
    n_expert = lax.axis_size("expert")
    n_dp = lax.axis_size("dp")
    chips = n_tensor // 2
    experts, width, block = w_down.shape
    slots = hidden_saved.shape[2]
    most = slots // n_expert
    half = most // 2
    tokens, choices = routes.shape[2:]
    own = grad_out.shape[2]
    dims = (experts, n_expert, tokens, choices, most)
    me = lax.axis_index("tensor")
    place = jnp.stack([lax.axis_index("expert"), me // 2, me % 2]).astype(jnp.int32)
    pair = [(i, i ^ 1) for i in range(n_tensor)]
    params = pltpu.CompilerParams(vmem_limit_bytes=50 * 1024 * 1024)

    work = 2 * experts * slots * width * block + 2 * n_expert * slots * tokens * block
    cost = pl.CostEstimate(flops=work, bytes_accessed=2 * w_down.size, transcendentals=0)

    w_other = lax.ppermute(w_down, "tensor", pair)
    first = me * (slots // n_tensor)
    my_hidden = lax.dynamic_slice_in_dim(hidden_saved[0], first, slots // n_tensor, 1)

    send = grad_out[0, 0].reshape(own, n_tensor, block).transpose(1, 0, 2)
    column = lax.all_to_all(send, "tensor", 0, 0, tiled=True).reshape(tokens, block)
    packed = jnp.concatenate([column, routes[0, 0].T.astype(BF), gates[0, 0].T], 0)
    packed = jnp.broadcast_to(packed[None], (n_expert,) + packed.shape)
    tok = lax.all_to_all(packed, "expert", 0, 0, tiled=True)
    vmem = pl.BlockSpec(memory_space=pltpu.VMEM)
    scaled_hot, hot, gate_col = pl.pallas_call(
        functools.partial(pick_kernel, dims=dims),
        out_shape=(
            jax.ShapeDtypeStruct((n_expert, experts * most, tokens), BF),
            jax.ShapeDtypeStruct((n_expert, experts * half, tokens), BF),
            jax.ShapeDtypeStruct((experts * half, 128), F32),
        ),
        grid_spec=pltpu.PrefetchScalarGridSpec(
            num_scalar_prefetch=1,
            grid=(1,),
            in_specs=[vmem],
            out_specs=(
                vmem,
                vmem,
                vmem,
            ),
        ),
        compiler_params=pltpu.CompilerParams(vmem_limit_bytes=16 * 1024 * 1024),
        cost_estimate=cost,
        name="pick",
    )(place, tok)
    other = lax.ppermute(tok, "tensor", pair)

    per = 2
    per_expert = lambda *shape: pl.BlockSpec((per,) + shape, lambda x: (x, 0, 0))
    block_f = width // n_dp
    pairs = chips // 2
    per_expert_p = lambda low, *shape: pl.BlockSpec((per,) + shape, lambda x, p: (x + low // per, 0, 0))

    def hidden_parts(low, count, hot):
        out = jax.ShapeDtypeStruct((pairs, count, half, width), BF)
        return pl.pallas_call(
            functools.partial(part_kernel, low=low, half=half),
            out_shape=(out, out),
            grid_spec=pltpu.PrefetchScalarGridSpec(
                num_scalar_prefetch=1,
                grid=(count // per,),
                in_specs=[
                    vmem,
                    vmem,
                    vmem,
                    per_expert_p(low, width, block),
                    per_expert_p(low, width, block),
                ],
                out_specs=(pl.BlockSpec((pairs, per, half, width), lambda x, p: (0, x, 0, 0)),) * 2,
                scratch_shapes=[pltpu.VMEM((count, slots // 2, block), F32)] * 2,
            ),
            compiler_params=pltpu.CompilerParams(vmem_limit_bytes=48 * 1024 * 1024),
            cost_estimate=cost,
            name="hidden_part",
        )(place, tok, other, hot, w_down, w_other)

    def swap(shift):
        at = lambda z: (z ^ 1) if shift == 0 else ((((z + 1) % chips) ^ 1) - 1) % chips
        return [(2 * z + c, 2 * at(z) + c) for z in range(chips) for c in range(2)]

    split = experts - per
    keep_a, near = hidden_parts(0, split, hot)
    near_back = lax.ppermute(near, "tensor", swap(0))
    scaled_hot, _ = lax.optimization_barrier((scaled_hot, near))
    partial = pl.pallas_call(
        weight_kernel,
        out_shape=jax.ShapeDtypeStruct((n_dp, experts, block_f, block), BF),
        grid=(experts // 4,),
        in_specs=[vmem, vmem, pl.BlockSpec((4, slots, width), lambda x: (x, 0, 0))],
        out_specs=pl.BlockSpec((n_dp, 4, block_f, block), lambda x: (0, x, 0, 0)),
        scratch_shapes=[pltpu.VMEM((experts, slots, block), BF)],
        compiler_params=params,
        cost_estimate=cost,
        name="weight_part",
    )(tok, scaled_hot, hidden_saved[0])
    total = lax.psum_scatter(partial, "dp", scatter_dimension=0, tiled=True)[0]
    hot_late, _ = lax.optimization_barrier((hot, partial))
    keep_b, far = hidden_parts(split, experts - split, hot_late)
    far_back = lax.ppermute(far, "tensor", swap(1))
    row = lambda n: pl.BlockSpec((2, n, half, width), lambda m: (m, 0, 0, 0))
    parts = pl.pallas_call(
        add_kernel,
        out_shape=jax.ShapeDtypeStruct((pairs, experts, half, width), BF),
        grid=(pairs // 2,),
        in_specs=[row(split), row(experts - split), row(split), row(experts - split)],
        out_specs=row(experts),
        compiler_params=params,
        cost_estimate=pl.CostEstimate(flops=42000000000, bytes_accessed=0, transcendentals=0),
        name="pair_sum",
    )(keep_a, keep_b, near_back, far_back)
    same_kind = [
        [2 * (2 * m + p) + c for m in range(pairs)] for p in range(2) for c in range(2)
    ]
    parts = lax.all_to_all(parts, "tensor", 0, 0, tiled=True, axis_index_groups=same_kind)
    grad_hidden, grad_gates = pl.pallas_call(
        finish_kernel,
        out_shape=(
            jax.ShapeDtypeStruct((experts, half, width), BF),
            jax.ShapeDtypeStruct((experts, half), F32),
        ),
        in_specs=[pl.BlockSpec(memory_space=pltpu.VMEM)] * 3,
        out_specs=(pl.BlockSpec(memory_space=pltpu.VMEM),) * 2,
        compiler_params=pltpu.CompilerParams(vmem_limit_bytes=32 * 1024 * 1024),
        name="finish",
    )(parts, gate_col, my_hidden)
    return grad_hidden[None], grad_gates[None], total


def solution(mesh):
    in_specs = (
        P("dp", "expert", "tensor", None),
        P("dp", "expert", None, None),
        P("dp", "expert", None, None),
        P("dp", "expert", None, None),
        P("expert", None, "tensor"),
    )
    out_specs = (
        P("dp", "expert", "tensor", None),
        P("dp", "expert", "tensor"),
        P("expert", "dp", "tensor"),
    )
    return jax.shard_map(local, mesh=mesh, in_specs=in_specs, out_specs=out_specs, check_vma=False)
```
